32 devices in a mesh: groups: 2 (over y), dap: 4 (over z), sub: 4 (over x, core).
Axes of the slice: x: 2, y: 2, z: 4, core: 2. Of those that a mesh axis runs over, the one named last changes fastest.
Arguments:
- pair: bfloat16 [128, 64, 128], P(('groups', 'dap', 'sub')), parts along dimension 0, may hold values from -6 to 6
- cotangent: bfloat16 [128, 64, 128], P(('groups', 'dap', 'sub')), parts along dimension 0, may hold values from -6 to 6
- residue_mask: int32 [128], P('groups'), parts along dimension 0, may hold values 0 or 1
- chain_labels: int32 [128], P('groups'), parts along dimension 0, may hold values from 0 to 3, never falling along the last dimension, each value on 1 to 32 neighbouring positions
- gain: float32 [128], replicated, may hold values from 0.5 to 1.5
- projection_weight: bfloat16 [4, 128, 128], replicated, may hold values from -0.5 to 0.5
- bias_weight: bfloat16 [128, 4], replicated, may hold values from -0.5 to 0.5
- output_weight: bfloat16 [128, 128], replicated, may hold values from -0.5 to 0.5
- position_bias_table: float32 [4, 66], replicated, may hold values from -4 to 240
- adapter_down_maps: bfloat16 [4, 128, 16], replicated, may hold values from -0.5 to 0.5
- adapter_up_maps: bfloat16 [4, 16, 128], replicated, may hold values from -1.5 to 1.5
Outputs:
- pair_grad: bfloat16 [128, 64, 128], P(('groups', 'dap', 'sub')), parts along dimension 0
- down_grad: float32 [8, 128, 16], P('groups'), parts along dimension 0
- up_grad: float32 [8, 16, 128], P('groups'), parts along dimension 0
The draws below stay inside these ranges and needn't reach their ends.
There are 2 independent parts, one for each index of `groups`. The reference program is written for one: setup_inputs(seed, part) draws one part's arguments, and reference() takes and returns one part's arrays. A program takes and returns all parts, laid end to end along the dimension named above; an argument that names none is the same for every part. Nothing has to cross between parts.
All inputs are finite; a program needn't handle non-finite values.
Results may differ from the reference program's by a relative error of at most 0.015.
The reference program's roundings to bfloat16 on the way count: a program that leaves them out, or rounds other values in their place, can miss the bound.
Values may be sent and summed in bfloat16 or wider, within the bound.
No kernel may reach another device: no remote copies, remote signals or barrier semaphores. Data moves between devices by JAX's collectives and lax.ppermute only.
A program may use at most 64 MiB of HBM per device.

```python
import math
import jax
import jax.numpy as jnp
import numpy as np
from jax import lax

PAIR_CHANNELS = 128
HEADS = 4
ADAPTER_RANK = 16
REL = 32
CHAINS = 4
N = 64


def draw_position_bias_table(key, part):
    key = jax.random.fold_in(key, 11)
    base_key = jax.random.fold_in(key, 0)
    bin_count = 2 * REL + 2
    table = jnp.clip(jax.random.normal(base_key, (HEADS, bin_count), jnp.float32), -4.0, 4.0)
    return table


def place_ends(drawn, rng, low, top_value):
    place = [jax.random.randint(jax.random.fold_in(rng, axis), (), 0, length) for axis, length in enumerate(drawn.shape)]
    main_axis = drawn.shape.index(max(drawn.shape))
    next_to = place[:main_axis] + [(place[main_axis] + 1) % drawn.shape[main_axis]] + place[main_axis + 1:]
    return drawn.at[tuple(place)].set(low).at[tuple(next_to)].set(top_value)


def block_levels(stream_key, dims, pieces, low, high):
    level, own = 1.0, jax.random.fold_in(stream_key, 6)
    for position, blocks in pieces:
        heights = jnp.exp(jax.random.uniform(jax.random.fold_in(own, position), (blocks,), jnp.float32, low / len(pieces), high / len(pieces)))
        level = level * jnp.repeat(heights, dims[position] // blocks).reshape([-1 if axis == position else 1 for axis in range(len(dims))])
    return level


def length_profile(number_of, total, limit, slope):
    portions = [(1 << 20) // math.isqrt(standing ** slope) + 1 for standing in range(2, number_of + 1)]
    rest, given = total - limit - (number_of - 1), [1] * (number_of - 1)
    while rest > 0:
        free = [i for i in range(number_of - 1) if given[i] < limit]
        mass, remaining = sum([portions[i] for i in free]), rest
        for i in free:
            addition = min(limit - given[i], max(1, remaining * portions[i] // mass), rest)
            given[i] = given[i] + addition
            rest = rest - addition
    return np.array([limit] + given)


def ragged(stream_key, count, total, reach, slope):
    if count == 2:
        one = jax.random.randint(stream_key, (), max(1, total - reach), min(reach, total - 1) + 1)
        return jnp.stack([one, total - one])
    sizes = jnp.asarray(length_profile(count, total, reach, slope), jnp.int32)
    twos = (count - 1) // 2
    giver, receiver = sizes[1:1 + 2 * twos:2], sizes[2:2 + 2 * twos:2]
    margin = jnp.minimum(giver - 1, reach - receiver)
    shifted = jax.random.randint(jax.random.fold_in(stream_key, 1), (twos,), 0, 1 << 20) % (margin + 1)
    sizes = sizes.at[1:1 + 2 * twos:2].set(giver - shifted).at[2:2 + 2 * twos:2].set(receiver + shifted)
    return sizes[jax.random.permutation(jax.random.fold_in(stream_key, 2), count)]


def bell_draw(own_key, shape, deviation, limit, cuts=(), held_as=jnp.bfloat16):
    values = deviation * jax.random.normal(own_key, shape, jnp.float32)
    if cuts:
        values = values * block_levels(own_key, shape, cuts, -0.22, 0.18)
    return jnp.clip(values, -limit, limit).astype(held_as)


def setup_inputs(seed: int = 0, part: int = 0) -> dict:
    streams_of = jax.random.split(jax.random.key(seed), 12)
    own_keys = jax.random.split(jax.random.fold_in(streams_of[11], part), 12)
    pair = bell_draw(own_keys[0], (N, N, PAIR_CHANNELS), 1.0, 6.0, ((0, 16),))
    cotangent = bell_draw(own_keys[1], (N, N, PAIR_CHANNELS), 1.0, 6.0, ((0, 16),))
    residue_mask = place_ends((jax.random.randint(own_keys[2], (N,), 0, 8) < 7).astype(jnp.int32), jax.random.fold_in(own_keys[2], 1), 0, 1)
    chain_labels = jnp.searchsorted(jnp.cumsum(ragged(own_keys[3], CHAINS, N, N // 2, 1)), jnp.arange(N), side="right").astype(jnp.int32)
    gain = jnp.clip(1.0 + 0.1 * jax.random.normal(streams_of[4], (PAIR_CHANNELS,), jnp.float32), 0.5, 1.5)
    projection_weight = bell_draw(streams_of[5], (4, PAIR_CHANNELS, PAIR_CHANNELS), PAIR_CHANNELS ** -0.5, 0.5)
    bias_weight = bell_draw(streams_of[6], (PAIR_CHANNELS, HEADS), PAIR_CHANNELS ** -0.5, 0.5)
    output_weight = bell_draw(streams_of[7], (PAIR_CHANNELS, PAIR_CHANNELS), PAIR_CHANNELS ** -0.5, 0.5)
    position_bias_table = draw_position_bias_table(jax.random.fold_in(streams_of[11], 71), part)
    adapter_down_maps = bell_draw(streams_of[9], (4, PAIR_CHANNELS, ADAPTER_RANK), PAIR_CHANNELS ** -0.5, 0.5)
    adapter_up_maps = bell_draw(streams_of[10], (4, ADAPTER_RANK, PAIR_CHANNELS), ADAPTER_RANK ** -0.5, 1.5)
    return {"pair": pair, "cotangent": cotangent, "residue_mask": residue_mask, "chain_labels": chain_labels, "gain": gain, "projection_weight": projection_weight, "bias_weight": bias_weight, "output_weight": output_weight, "position_bias_table": position_bias_table, "adapter_down_maps": adapter_down_maps, "adapter_up_maps": adapter_up_maps}


epsilon = 1e-05

def rounded(values):
    return lax.optimization_barrier(values.astype(jnp.bfloat16)).astype(jnp.float32)

def normalize(pair_rows, gain):
    widened = pair_rows.astype(jnp.float32)
    average = lax.optimization_barrier(jnp.mean(widened, axis=-1, keepdims=True))
    centred = widened - average
    spread = lax.optimization_barrier(jnp.mean(centred * centred, axis=-1, keepdims=True))
    return centred * lax.rsqrt(spread + epsilon) * gain

def relative_bias(chain_labels, row_start, row_count, position_bias_table):
    key_count = chain_labels.shape[0]
    bin_count = position_bias_table.shape[1]
    reach_max = (bin_count - 2) // 2
    query_pos = row_start + jnp.arange(row_count, dtype=jnp.int32)
    key_pos = jnp.arange(key_count, dtype=jnp.int32)
    query_chain = lax.dynamic_slice_in_dim(chain_labels, row_start, row_count)
    same_chain = query_chain[:, None] == chain_labels[None, :]
    offset = jnp.clip(key_pos[None, :] - query_pos[:, None], -reach_max, reach_max) + reach_max
    bin_index = jnp.where(same_chain, offset, bin_count - 1)
    onehot = (bin_index[:, :, None] == jnp.arange(bin_count, dtype=jnp.int32)[None, None, :]).astype(jnp.float32)
    return jnp.einsum('rkb,hb->hrk', onehot, position_bias_table, precision=lax.Precision.HIGHEST)

def row_attention(layer_normed_row, complete_bias, key_valid_mask, projection_weight, output_weight, adapter_down_maps, adapter_up_maps):
    key_count, channel_count = layer_normed_row.shape
    head_count = complete_bias.shape[0]
    head_width = channel_count // head_count
    score_scale = 1.0 / math.sqrt(head_width)

    def adapted(projection_index):
        frozen_term = jnp.dot(layer_normed_row.astype(jnp.bfloat16), projection_weight[projection_index], preferred_element_type=jnp.float32)
        reduced_update = jnp.dot(layer_normed_row.astype(jnp.bfloat16), adapter_down_maps[projection_index].astype(jnp.bfloat16), preferred_element_type=jnp.float32).astype(jnp.bfloat16)
        return frozen_term + jnp.dot(reduced_update, adapter_up_maps[projection_index].astype(jnp.bfloat16), preferred_element_type=jnp.float32)
    queries = rounded(adapted(0)).reshape(key_count, head_count, head_width)
    keys_all = rounded(adapted(1)).reshape(key_count, head_count, head_width)
    values_all = rounded(adapted(2)).reshape(key_count, head_count, head_width)
    scores = jnp.einsum('jhd,khd->hjk', queries, keys_all) * score_scale + complete_bias
    scores = jnp.where(key_valid_mask[None, None, :], scores, -1000000000.0)
    weights = jax.nn.softmax(scores, axis=-1)
    attended = jnp.einsum('hjk,khd->jhd', rounded(weights), values_all).reshape(key_count, channel_count)
    gating = jax.nn.sigmoid(jnp.dot(layer_normed_row.astype(jnp.bfloat16), projection_weight[3], preferred_element_type=jnp.float32))
    gated_output = (gating * attended).astype(jnp.bfloat16)
    reduced_output = jnp.dot(gated_output, adapter_down_maps[3].astype(jnp.bfloat16), preferred_element_type=jnp.float32).astype(jnp.bfloat16)
    return jnp.dot(gated_output, output_weight, preferred_element_type=jnp.float32) + jnp.dot(reduced_output, adapter_up_maps[3].astype(jnp.bfloat16), preferred_element_type=jnp.float32)

def reference(pair, cotangent, residue_mask, chain_labels, gain, projection_weight, bias_weight, output_weight, position_bias_table, adapter_down_maps, adapter_up_maps):
    key_valid_mask = residue_mask > 0
    residue_count = pair.shape[0]
    rel_bias = relative_bias(chain_labels, jnp.int32(0), residue_count, position_bias_table)

    def forward_pass(pair_in, down_matrix, up_matrix):
        columns_in = jnp.transpose(pair_in, (1, 0, 2))
        normed = normalize(columns_in, gain)
        projected = jnp.einsum('jkc,ch->hjk', rounded(normed), bias_weight.astype(jnp.float32))
        pair_bias = (projected + rel_bias).astype(jnp.bfloat16)
        complete_bias = lax.optimization_barrier(pair_bias).astype(jnp.float32)

        def one_row(layer_normed_row):
            return row_attention(layer_normed_row, complete_bias, key_valid_mask, projection_weight, output_weight, down_matrix, up_matrix)
        results = lax.map(jax.checkpoint(one_row), normed)
        return jnp.transpose(results, (1, 0, 2))
    unused_value, vector_jacobian = jax.vjp(forward_pass, pair, adapter_down_maps.astype(jnp.float32), adapter_up_maps.astype(jnp.float32))
    pair_grad, down_grad, up_grad = vector_jacobian(cotangent.astype(jnp.float32))
    return (pair_grad, down_grad, up_grad)
```

```python
import functools
import math

import jax
import jax.numpy as jnp
from jax import lax
from jax.experimental import pallas as pl
from jax.experimental.pallas import tpu as pltpu
from jax.sharding import PartitionSpec as P

epsilon = 1e-05
lanes = 128
block = 256
masked_bias = -3e38
group_axes = ("dap", "sub")
vmem = pl.BlockSpec(memory_space=pltpu.VMEM)
smem = pl.BlockSpec(memory_space=pltpu.SMEM)


def nn(left, right):
    return jnp.dot(left, right, preferred_element_type=jnp.float32)


def nt(left, right):
    return lax.dot_general(left, right, (((1,), (1,)), ((), ())), preferred_element_type=jnp.float32)


def tn(left, right):
    return lax.dot_general(left, right, (((0,), (0,)), ((), ())), preferred_element_type=jnp.float32)


def half(values):
    return values.astype(jnp.bfloat16)


def repeat(count, body):
    if count == 1:
        body(0)
    else:
        lax.fori_loop(0, count, lambda step, carry: (body(step), carry)[1], 0)


def before_kernel(
    mask_ref, label_ref, label_row_ref, pair_ref, cot_ref, gain_ref, bias_weight_ref, table_ref,
    send_ref, unit_ref, inverse_ref, normed_ref, cells_ref, bias_ref,
):
    own, count, channels = pair_ref.shape
    peers = count // own
    heads, bins = table_ref.shape
    reach = (bins - 2) // 2
    first = lax.axis_index(group_axes) * own
    bias_rows = heads * count // lanes
    gain = gain_ref[...]
    key_pos = lax.broadcasted_iota(jnp.int32, (1, count), 1)
    bin_ids = lax.broadcasted_iota(jnp.int32, (bins, count), 0)
    for row in range(own):
        here = first + row
        values = pair_ref[row].astype(jnp.float32)
        centred = values - jnp.mean(values, axis=-1, keepdims=True)
        inverse = lax.rsqrt(jnp.mean(centred * centred, axis=-1, keepdims=True) + epsilon)
        unit = centred * inverse
        normed = unit * gain
        unit_ref[row * count : (row + 1) * count] = unit
        inverse_ref[row * count : (row + 1) * count] = inverse
        normed_ref[row * count : (row + 1) * count] = normed
        same = label_row_ref[...] == label_ref[here]
        offset = jnp.clip(here - key_pos, -reach, reach) + reach
        onehot = (bin_ids == jnp.where(same, offset, bins - 1)).astype(jnp.float32)
        relative = lax.dot_general(
            table_ref[...], onehot, (((1,), (0,)), ((), ())),
            precision=lax.Precision.HIGHEST, preferred_element_type=jnp.float32,
        )
        bias = half(nt(bias_weight_ref[...], half(normed)) + relative).astype(jnp.float32)
        bias = jnp.where(mask_ref[here] > 0, bias, masked_bias)
        for head in range(heads):
            if count < lanes:
                each = lanes // count
                place = (head % each) * count
                bias_ref[row * bias_rows + head // each, place : place + count] = bias[head]
            else:
                for part in range(count // lanes):
                    bias_ref[row * bias_rows + head * (count // lanes) + part, :] = bias[
                        head, part * lanes : (part + 1) * lanes
                    ]
    cell_rows = own * own

    def scatter():
        for row in range(own):
            for place in range(own):
                cells_ref[pl.ds(row * own + place, peers, stride=cell_rows)] = normed_ref[
                    pl.ds(row * count + place, peers, stride=own)
                ]
        return half(cells_ref[...]).reshape(peers, cell_rows, channels)

    send_ref[:, 0:cell_rows] = scatter()
    for row in range(own):
        normed_ref[row * count : (row + 1) * count] = cot_ref[row].astype(jnp.float32)
    send_ref[:, cell_rows : 2 * cell_rows] = scatter()
    bias_all = half(bias_ref[...])
    send_ref[:, 2 * cell_rows :] = jnp.broadcast_to(bias_all[None], (peers, *bias_all.shape))


def middle_kernel(
    recv_ref, weight_ref, out_weight_ref, down_ref, up_ref,
    send_ref,
    rows_ref, x_ref, u_ref, bias_ref, q_ref, k_ref, v_ref, da_ref, gate_ref, dgated_ref,
    att_ref, dq_ref, dk_ref, dv_ref, bias_grad_ref, adapter_ref,
    *, own, heads, sent,
):
    peers = recv_ref.shape[0]
    channels = recv_ref.shape[2]
    count = own * peers
    cell_rows = own * own
    width = channels // heads
    scale = 1.0 / math.sqrt(width)
    rank = down_ref.shape[1]
    bias_rows = heads * count // lanes
    total = own * count
    joint = min(count, block)
    joint_heads = block // joint

    for target, offset in ((x_ref, 0), (u_ref, cell_rows)):
        rows_ref[...] = recv_ref[:, offset : offset + cell_rows].astype(jnp.float32).reshape(total, channels)
        for place in range(own):
            target[place * count : (place + 1) * count] = half(rows_ref[pl.ds(place, count, stride=own)])
    gathered = recv_ref[:, 2 * cell_rows :].astype(jnp.float32)
    bias_grad_ref[...] = gathered.reshape(count * bias_rows, lanes)
    for part in range(bias_rows):
        bias_ref[:, part * lanes : (part + 1) * lanes] = bias_grad_ref[pl.ds(part, count, stride=bias_rows)]

    weights = [weight_ref[index] for index in range(4)]
    downs = [down_ref[index] for index in range(4)]
    ups = [up_ref[index] for index in range(4)]

    def project(step):
        rows = pl.ds(pl.multiple_of(step * block, block), block)
        x = x_ref[rows]
        u = u_ref[rows]
        for index, target in enumerate((q_ref, k_ref, v_ref)):
            low = half(nt(x, downs[index]))
            target[rows] = half(nn(x, weights[index]) + nn(low, ups[index]))
        gate = jax.nn.sigmoid(nn(x, weights[3]))
        dgated = half(nt(u, out_weight_ref[...]) + nn(half(nt(u, ups[3])), downs[3])).astype(jnp.float32)
        gate_ref[rows] = gate
        dgated_ref[rows] = dgated
        da_ref[rows] = half(dgated * gate)

    repeat(total // block, project)

    head_of = lax.broadcasted_iota(jnp.int32, (1, channels), 1) // width
    blocks = heads * count // block

    def attend(row, part):
        start = part * block // count
        column = pl.multiple_of(part * block, block)
        first = 0 if count <= block else pl.multiple_of(lax.rem(part * block, count), block)
        queries = pl.ds(row * count + first, joint)
        keys = pl.ds(row * count, count)
        spots = [(head_of == start + head).astype(jnp.float32) for head in range(joint_heads)]

        def spread(values):
            return jnp.concatenate([values * half(spot) for spot in spots], axis=0)

        def collect(values):
            return sum(values[head * joint : (head + 1) * joint] * spots[head] for head in range(joint_heads))

        q_wide = spread(q_ref[queries])
        da_wide = spread(da_ref[queries])
        k_all = k_ref[keys]
        v_all = v_ref[keys]
        bias = bias_ref[:, pl.ds(column, block)]
        valid = bias > -1e38
        scores = jnp.where(valid, nt(k_all, q_wide) * scale + bias, -1000000000.0)
        powers = jnp.exp(scores - jnp.max(scores, axis=0, keepdims=True))
        chances = powers / jnp.sum(powers, axis=0, keepdims=True)
        rounded = half(chances)
        dchances = half(nt(v_all, da_wide)).astype(jnp.float32)
        inner = dchances * chances
        dscores = inner - chances * jnp.sum(inner, axis=0, keepdims=True)
        dscores = jnp.where(valid, dscores, 0.0)
        scaled = half(dscores * scale)
        return (
            queries, keys, column,
            collect(tn(rounded, v_all)), collect(tn(scaled, k_all)),
            nn(scaled, q_wide), nn(rounded, da_wide), dscores,
        )

    if blocks == 1:
        bias_grad = None
        for row in range(own):
            queries, keys, column, att, dq, dk, dv, dscores = attend(row, 0)
            att_ref[queries] = att
            dq_ref[queries] = dq
            dk_ref[keys] = dk
            dv_ref[keys] = dv
            bias_grad = dscores if bias_grad is None else bias_grad + dscores
        bias_ref[...] = bias_grad
    else:
        bias_sum_ref = bias_grad_ref
        for ref in (att_ref, dq_ref, dk_ref, dv_ref):
            ref[...] = jnp.zeros_like(ref)

        def each(part):
            def each_row(row, bias_grad):
                queries, keys, column, att, dq, dk, dv, dscores = attend(row, part)
                att_ref[queries] += att
                dq_ref[queries] += dq
                dk_ref[keys] += dk
                dv_ref[keys] += dv
                return bias_grad + dscores

            bias_grad = lax.fori_loop(0, own, each_row, jnp.zeros((count, block), jnp.float32))
            bias_ref[:, pl.ds(pl.multiple_of(part * block, block), block)] = bias_grad

        repeat(blocks, each)
    for part in range(bias_rows):
        bias_grad_ref[pl.ds(part, count, stride=bias_rows)] = bias_ref[:, part * lanes : (part + 1) * lanes]

    adapter_ref[...] = jnp.zeros_like(adapter_ref)

    def finish(step):
        rows = pl.ds(pl.multiple_of(step * block, block), block)
        x = x_ref[rows]
        u = u_ref[rows]
        att = att_ref[rows]
        gate = gate_ref[rows]
        dgated = dgated_ref[rows]
        gated = half(gate * att)
        dgate = half(dgated * att * (gate * (1.0 - gate)))
        low_out = half(nt(downs[3], gated))
        dlow_out = half(nt(ups[3], u))
        downs_grad = [None] * 3 + [nn(dlow_out, gated)]
        ups_grad = [None] * 3 + [nn(low_out, u)]
        grad = nt(dgate, weights[3])
        for index, source in enumerate((dq_ref, dk_ref, dv_ref)):
            dproj = half(source[rows])
            ups_grad[index] = nn(half(nt(downs[index], x)), dproj)
            downs_grad[index] = nn(half(nt(ups[index], dproj)), x)
            grad = grad + nt(dproj, weights[index]) + nn(half(nt(dproj, ups[index])), downs[index])
        for index in range(4):
            adapter_ref[index * rank : (index + 1) * rank] += downs_grad[index]
            adapter_ref[(4 + index) * rank : (5 + index) * rank] += ups_grad[index]
        rows_ref[rows] = grad

    repeat(total // block, finish)

    for row in range(own):
        for place in range(own):
            send_ref[pl.ds(row * own + place, peers, stride=sent)] = rows_ref[
                pl.ds(place * count + row, peers, stride=own)
            ]
    bias_chunk = own * bias_rows
    adapter_chunk = adapter_ref.shape[0] // peers
    for peer in range(peers):
        base = peer * sent + cell_rows
        send_ref[base : base + bias_chunk] = bias_grad_ref[peer * bias_chunk : (peer + 1) * bias_chunk]
        base = base + bias_chunk
        send_ref[base : base + adapter_chunk] = adapter_ref[peer * adapter_chunk : (peer + 1) * adapter_chunk]


def adapter_kernel(recv_ref, send_ref, *, offset):
    peers = recv_ref.shape[0]
    chunk = send_ref.shape[1]
    send_ref[...] = jnp.broadcast_to(
        jnp.sum(recv_ref[:, offset : offset + chunk], axis=0, keepdims=True), send_ref.shape
    )


def after_kernel(
    recv_ref, unit_ref, inverse_ref, gain_ref, bias_weight_ref, out_ref, rows_ref, bias_ref, *, sent
):
    own, count, channels = out_ref.shape
    peers = count // own
    heads = bias_weight_ref.shape[0]
    cell_rows = own * own
    bias_rows = heads * count // lanes
    for row in range(own):
        for place in range(own):
            rows_ref[pl.ds(row * count + place, peers, stride=own)] = recv_ref[
                pl.ds(row * own + place, peers, stride=sent)
            ]
    summed = recv_ref[cell_rows : cell_rows + own * bias_rows]
    for peer in range(1, peers):
        base = peer * sent + cell_rows
        summed = summed + recv_ref[base : base + own * bias_rows]
    bias_ref[...] = summed
    for row in range(own):
        pieces = []
        for head in range(heads):
            if count < lanes:
                each = lanes // count
                place = (head % each) * count
                line = row * bias_rows + head // each
                pieces.append(bias_ref[line : line + 1, place : place + count])
            else:
                parts = count // lanes
                line = row * bias_rows + head * parts
                pieces.append(
                    jnp.concatenate([bias_ref[line + part : line + part + 1] for part in range(parts)], axis=1)
                )
        bias_grad = half(jnp.concatenate(pieces, axis=0))
        rows = slice(row * count, (row + 1) * count)
        unit = unit_ref[rows]
        grad = (rows_ref[rows] + tn(bias_grad, bias_weight_ref[...])) * gain_ref[...]
        along = jnp.mean(grad * unit, axis=-1, keepdims=True)
        result = inverse_ref[rows] * (grad - jnp.mean(grad, axis=-1, keepdims=True) - unit * along)
        out_ref[row] = half(result)


def exchange(values):
    return lax.all_to_all(values, group_axes, split_axis=0, concat_axis=0, tiled=True)


def local(
    pair,
    cotangent,
    residue_mask,
    chain_labels,
    gain,
    projection_weight,
    bias_weight,
    output_weight,
    position_bias_table,
    adapter_down_maps,
    adapter_up_maps,
):
    own, count, channels = pair.shape
    peers = count // own
    heads = position_bias_table.shape[0]
    rank = adapter_up_maps.shape[1]
    total = own * count
    cell_rows = own * own
    bias_rows = heads * count // lanes
    adapter_rows = 8 * rank
    adapter_chunk = adapter_rows // peers
    bias_chunk = own * bias_rows
    sent = -(-(cell_rows + bias_chunk + adapter_chunk) // 8) * 8
    f32, bf16 = jnp.float32, jnp.bfloat16
    gain_row = gain.reshape(1, channels)
    bias_weight_t = bias_weight.T
    downs = jnp.swapaxes(adapter_down_maps, 1, 2)
    params = pltpu.CompilerParams(vmem_limit_bytes=56 * 1024 * 1024)

    first_send, unit, inverse = pl.pallas_call(
        before_kernel,
        out_shape=(
            jax.ShapeDtypeStruct((peers, 2 * cell_rows + bias_chunk, channels), bf16),
            jax.ShapeDtypeStruct((total, channels), f32),
            jax.ShapeDtypeStruct((total, 1), f32),
        ),
        in_specs=[smem, smem] + [vmem] * 6,
        out_specs=(vmem, vmem, vmem),
        scratch_shapes=[
            pltpu.VMEM((total, channels), f32),
            pltpu.VMEM((total, channels), f32),
            pltpu.VMEM((bias_chunk, lanes), f32),
        ],
        compiler_params=params,
        name="before",
    )(
        residue_mask, chain_labels, chain_labels.reshape(1, count), pair, cotangent, gain_row,
        bias_weight_t, position_bias_table,
    )
    first_recv = exchange(first_send)
    second_send = pl.pallas_call(
        functools.partial(middle_kernel, own=own, heads=heads, sent=sent),
        out_shape=jax.ShapeDtypeStruct((peers * sent, channels), f32),
        in_specs=[vmem] * 5,
        out_specs=vmem,
        scratch_shapes=[
            pltpu.VMEM((total, channels), f32),
            pltpu.VMEM((total, channels), bf16),
            pltpu.VMEM((total, channels), bf16),
            pltpu.VMEM((count, heads * count), f32),
            *[pltpu.VMEM((total, channels), bf16)] * 4,
            *[pltpu.VMEM((total, channels), f32)] * 6,
            pltpu.VMEM((count * bias_rows, lanes), f32),
            pltpu.VMEM((adapter_rows, channels), f32),
        ],
        compiler_params=params,
        name="middle",
    )(first_recv, projection_weight, output_weight, downs, adapter_up_maps)
    second_recv = exchange(second_send)
    third_send = pl.pallas_call(
        functools.partial(adapter_kernel, offset=cell_rows + bias_chunk),
        out_shape=jax.ShapeDtypeStruct((peers, adapter_chunk, channels), f32),
        in_specs=[vmem],
        out_specs=vmem,
        compiler_params=params,
        name="adapters",
    )(second_recv.reshape(peers, sent, channels))
    third_recv = exchange(third_send).reshape(2, 4, rank, channels)
    pair_grad = pl.pallas_call(
        functools.partial(after_kernel, sent=sent),
        out_shape=jax.ShapeDtypeStruct((own, count, channels), bf16),
        in_specs=[vmem] * 5,
        out_specs=vmem,
        scratch_shapes=[
            pltpu.VMEM((total, channels), f32),
            pltpu.VMEM((bias_chunk, lanes), f32),
        ],
        compiler_params=params,
        name="after",
    )(second_recv, unit, inverse, gain_row, bias_weight_t)
    return (pair_grad, jnp.swapaxes(third_recv[0], 1, 2), third_recv[1])


def solution(mesh):
    return jax.shard_map(
        local,
        mesh=mesh,
        in_specs=(
            P(("groups", "dap", "sub"), None, None),
            P(("groups", "dap", "sub"), None, None),
            P("groups"),
            P("groups"),
            P(),
            P(),
            P(),
            P(),
            P(),
            P(),
            P(),
        ),
        out_specs=(
            P(("groups", "dap", "sub"), None, None),
            P("groups", None, None),
            P("groups", None, None),
        ),
        check_vma=False,
    )
```

```python
import functools
import math

import jax
import jax.numpy as jnp
from jax import lax
from jax.experimental import pallas as pl
from jax.experimental.pallas import tpu as pltpu
from jax.sharding import PartitionSpec as P

epsilon = 1e-05
lanes = 128
block = 256
masked_bias = -3e38
group_axes = ("dap", "sub")
vmem = pl.BlockSpec(memory_space=pltpu.VMEM)
smem = pl.BlockSpec(memory_space=pltpu.SMEM)


def nn(left, right):
    return jnp.dot(left, right, preferred_element_type=jnp.float32)


def nt(left, right):
    return lax.dot_general(left, right, (((1,), (1,)), ((), ())), preferred_element_type=jnp.float32)


def tn(left, right):
    return lax.dot_general(left, right, (((0,), (0,)), ((), ())), preferred_element_type=jnp.float32)


def half(values):
    return values.astype(jnp.bfloat16)


def whole(values):
    return half(values).astype(jnp.float32)


def repeat(count, body):
    if count == 1:
        body(0)
    else:
        lax.fori_loop(0, count, lambda step, carry: (body(step), carry)[1], 0)


def before_kernel(
    mask_ref, label_ref, label_row_ref, pair_ref, cot_ref, gain_ref, bias_weight_ref, table_ref,
    send_ref, unit_ref, inverse_ref, normed_ref, cells_ref, bias_ref,
):
    own, count, channels = pair_ref.shape
    peers = count // own
    heads, bins = table_ref.shape
    reach = (bins - 2) // 2
    first = lax.axis_index(group_axes) * own
    bias_rows = heads * count // lanes
    gain = gain_ref[...]
    key_pos = lax.broadcasted_iota(jnp.int32, (1, count), 1)
    bin_ids = lax.broadcasted_iota(jnp.int32, (bins, count), 0)
    for row in range(own):
        here = first + row
        values = pair_ref[row].astype(jnp.float32)
        centred = values - jnp.mean(values, axis=-1, keepdims=True)
        inverse = lax.rsqrt(jnp.mean(centred * centred, axis=-1, keepdims=True) + epsilon)
        unit = centred * inverse
        normed = unit * gain
        unit_ref[row * count : (row + 1) * count] = unit
        inverse_ref[row * count : (row + 1) * count] = inverse
        normed_ref[row * count : (row + 1) * count] = normed
        same = label_row_ref[...] == label_ref[here]
        offset = jnp.clip(here - key_pos, -reach, reach) + reach
        onehot = (bin_ids == jnp.where(same, offset, bins - 1)).astype(jnp.float32)
        relative = lax.dot_general(
            table_ref[...], onehot, (((1,), (0,)), ((), ())),
            precision=lax.Precision.HIGHEST, preferred_element_type=jnp.float32,
        )
        bias = half(nt(bias_weight_ref[...], half(normed)) + relative).astype(jnp.float32)
        bias = jnp.where(mask_ref[here] > 0, bias, masked_bias)
        for head in range(heads):
            if count < lanes:
                each = lanes // count
                place = (head % each) * count
                bias_ref[row * bias_rows + head // each, place : place + count] = bias[head]
            else:
                for part in range(count // lanes):
                    bias_ref[row * bias_rows + head * (count // lanes) + part, :] = bias[
                        head, part * lanes : (part + 1) * lanes
                    ]
    cell_rows = own * own

    def scatter():
        for row in range(own):
            for place in range(own):
                cells_ref[pl.ds(row * own + place, peers, stride=cell_rows)] = normed_ref[
                    pl.ds(row * count + place, peers, stride=own)
                ]
        return half(cells_ref[...]).reshape(peers, cell_rows, channels)

    send_ref[:, 0:cell_rows] = scatter()
    for row in range(own):
        normed_ref[row * count : (row + 1) * count] = cot_ref[row].astype(jnp.float32)
    send_ref[:, cell_rows : 2 * cell_rows] = scatter()
    bias_all = half(bias_ref[...])
    send_ref[:, 2 * cell_rows :] = jnp.broadcast_to(bias_all[None], (peers, *bias_all.shape))


def middle_kernel(
    recv_ref, weight_ref, out_weight_ref, down_ref, up_ref,
    send_ref, keep_ref, give_ref,
    rows_ref, x_ref, u_ref, bias_ref, q_ref, k_ref, v_ref, da_ref, da2_ref, gate_ref, dgated_ref,
    att_ref, dq_ref, dk_ref, dv_ref, bias_grad_ref, adapter_ref, cells_ref,
    *, own, heads,
):
    peers = recv_ref.shape[0]
    channels = recv_ref.shape[2]
    count = own * peers
    cell_rows = own * own
    width = channels // heads
    scale = 1.0 / math.sqrt(width)
    rank = down_ref.shape[1]
    bias_rows = heads * count // lanes
    total = own * count
    joint = min(count, block)
    joint_heads = block // joint

    for target, offset in ((x_ref, 0), (u_ref, cell_rows)):
        rows_ref[...] = recv_ref[:, offset : offset + cell_rows].astype(jnp.float32).reshape(total, channels)
        for place in range(own):
            target[place * count : (place + 1) * count] = half(rows_ref[pl.ds(place, count, stride=own)])
    gathered = recv_ref[:, 2 * cell_rows :].astype(jnp.float32)
    bias_grad_ref[...] = gathered.reshape(count * bias_rows, lanes)
    for part in range(bias_rows):
        bias_ref[:, part * lanes : (part + 1) * lanes] = bias_grad_ref[pl.ds(part, count, stride=bias_rows)]

    weights = [weight_ref[index] for index in range(4)]
    downs = [down_ref[index] for index in range(4)]
    ups = [up_ref[index] for index in range(4)]

    def project(step):
        rows = pl.ds(pl.multiple_of(step * block, block), block)
        x = x_ref[rows]
        u = u_ref[rows]
        for index, target in enumerate((q_ref, k_ref, v_ref)):
            low = half(nt(x, downs[index]))
            target[rows] = half(nn(x, weights[index]) + nn(low, ups[index]))
        gate = jax.nn.sigmoid(nn(x, weights[3]))
        dgated = half(whole(nt(u, out_weight_ref[...])) + whole(nn(half(nt(u, ups[3])), downs[3]))).astype(jnp.float32)
        gate_ref[rows] = gate
        dgated_ref[rows] = dgated
        da_ref[rows] = half(dgated * gate)
        da2_ref[rows] = half(dgated * gate - half(dgated * gate).astype(jnp.float32))

    repeat(total // block, project)

    head_of = lax.broadcasted_iota(jnp.int32, (1, channels), 1) // width
    blocks = heads * count // block

    def attend(row, part):
        start = part * block // count
        column = pl.multiple_of(part * block, block)
        first = 0 if count <= block else pl.multiple_of(lax.rem(part * block, count), block)
        queries = pl.ds(row * count + first, joint)
        keys = pl.ds(row * count, count)
        spots = [(head_of == start + head).astype(jnp.float32) for head in range(joint_heads)]

        def spread(values):
            return jnp.concatenate([values * half(spot) for spot in spots], axis=0)

        def collect(values):
            return sum(values[head * joint : (head + 1) * joint] * spots[head] for head in range(joint_heads))

        q_wide = spread(q_ref[queries])
        da_wide = spread(da_ref[queries])
        da2_wide = spread(da2_ref[queries])
        k_all = k_ref[keys]
        v_all = v_ref[keys]
        bias = bias_ref[:, pl.ds(column, block)]
        valid = bias > -1e38
        scores = jnp.where(valid, nt(k_all, q_wide) * scale + bias, -1000000000.0)
        powers = jnp.exp(scores - jnp.max(scores, axis=0, keepdims=True))
        chances = powers / jnp.sum(powers, axis=0, keepdims=True)
        rounded = half(chances)
        dchances = half(nt(v_all, da_wide)+nt(v_all, da2_wide)).astype(jnp.float32)
        inner = dchances * chances
        dscores = inner - chances * jnp.sum(inner, axis=0, keepdims=True)
        dscores = jnp.where(valid, dscores, 0.0)
        scaled = half(dscores * scale)
        rest = half(dscores * scale - scaled.astype(jnp.float32))
        return (
            queries, keys, column,
            collect(tn(rounded, v_all)), collect(tn(scaled, k_all) + tn(rest, k_all)),
            nn(scaled, q_wide) + nn(rest, q_wide), nn(rounded, da_wide)+nn(rounded, da2_wide), dscores,
        )

    if blocks == 1:
        bias_grad = None
        for row in range(own):
            queries, keys, column, att, dq, dk, dv, dscores = attend(row, 0)
            att_ref[queries] = att
            dq_ref[queries] = dq
            dk_ref[keys] = dk
            dv_ref[keys] = dv
            bias_grad = dscores if bias_grad is None else bias_grad + dscores
        bias_ref[...] = bias_grad
    else:
        bias_sum_ref = bias_grad_ref
        for ref in (att_ref, dq_ref, dk_ref, dv_ref):
            ref[...] = jnp.zeros_like(ref)

        def each(part):
            def each_row(row, bias_grad):
                queries, keys, column, att, dq, dk, dv, dscores = attend(row, part)
                att_ref[queries] += att
                dq_ref[queries] += dq
                dk_ref[keys] += dk
                dv_ref[keys] += dv
                return bias_grad + dscores

            bias_grad = lax.fori_loop(0, own, each_row, jnp.zeros((count, block), jnp.float32))
            bias_ref[:, pl.ds(pl.multiple_of(part * block, block), block)] = bias_grad

        repeat(blocks, each)
    for part in range(bias_rows):
        bias_grad_ref[pl.ds(part, count, stride=bias_rows)] = bias_ref[:, part * lanes : (part + 1) * lanes]

    adapter_ref[...] = jnp.zeros_like(adapter_ref)

    def finish(step):
        rows = pl.ds(pl.multiple_of(step * block, block), block)
        x = x_ref[rows]
        u = u_ref[rows]
        att = att_ref[rows]
        gate = gate_ref[rows]
        dgated = dgated_ref[rows]
        gated = half(gate * att)
        dgate = half(dgated * att * (gate * (1.0 - gate)))
        low_out = half(nt(downs[3], gated))
        dlow_out = half(nt(ups[3], u))
        downs_grad = [None] * 3 + [nn(dlow_out, gated)]
        ups_grad = [None] * 3 + [nn(low_out, u)]
        grad = whole(nt(dgate, weights[3]))
        for index, source in enumerate((dq_ref, dk_ref, dv_ref)):
            dproj = half(source[rows])
            ups_grad[index] = nn(half(nt(downs[index], x)), dproj)
            downs_grad[index] = nn(half(nt(ups[index], dproj)), x)
            grad = grad + whole(nt(dproj, weights[index])) + whole(nn(half(nt(dproj, ups[index])), downs[index]))
        for index in range(4):
            adapter_ref[index * rank : (index + 1) * rank] += downs_grad[index]
            adapter_ref[(4 + index) * rank : (5 + index) * rank] += ups_grad[index]
        rows_ref[rows] = grad

    repeat(total // block, finish)

    bias_chunk = own * bias_rows
    for row in range(own):
        for place in range(own):
            cells_ref[pl.ds(row * own + place, peers, stride=cell_rows)] = rows_ref[
                pl.ds(place * count + row, peers, stride=own)
            ]
    send_ref[:, 0:cell_rows] = half(cells_ref[...]).reshape(peers, cell_rows, channels)
    send_ref[:, cell_rows:] = half(bias_grad_ref[...]).reshape(peers, bias_chunk, lanes)
    side = lax.rem(lax.axis_index("sub"), 2) == 0
    split = adapter_ref.shape[0] // 2
    keep_ref[...] = jnp.where(side, adapter_ref[:split], adapter_ref[split:])
    give_ref[...] = jnp.where(side, adapter_ref[split:], adapter_ref[:split])


def pack_kernel(cells_ref, keep_ref, taken_ref, send_ref):
    peers, rows, _ = cells_ref.shape
    send_ref[:, :rows] = cells_ref[...]
    summed = half(keep_ref[...] + taken_ref[...])
    quarter = summed.shape[0] // 2
    for peer in range(peers):
        side = peer % 2
        send_ref[peer, rows:] = summed[side * quarter : (side + 1) * quarter]


def adapter_kernel(recv_ref, out_ref, *, offset):
    quarter = out_ref.shape[0] // 2
    for side in range(2):
        total = recv_ref[side, offset:].astype(jnp.float32)
        for peer in range(side + 2, recv_ref.shape[0], 2):
            total = total + recv_ref[peer, offset:].astype(jnp.float32)
        out_ref[side * quarter : (side + 1) * quarter] = total


def after_kernel(
    recv_ref, mine_ref, theirs_ref, unit_ref, inverse_ref, gain_ref, bias_weight_ref,
    out_ref, down_ref, up_ref, rows_ref, cells_ref, bias_ref,
):
    own, count, channels = out_ref.shape
    peers = count // own
    heads = bias_weight_ref.shape[0]
    cell_rows = own * own
    bias_rows = heads * count // lanes
    side = lax.rem(lax.axis_index("sub"), 2) == 0
    quarter = mine_ref.shape[0] // 2
    for index, ref in enumerate((down_ref, up_ref)):
        mine = mine_ref[index * quarter : (index + 1) * quarter]
        theirs = theirs_ref[index * quarter : (index + 1) * quarter]
        ref[:quarter] = jnp.where(side, mine, theirs)
        ref[quarter:] = jnp.where(side, theirs, mine)
    cells_ref[...] = recv_ref[:, :cell_rows].astype(jnp.float32).reshape(own * count, channels)
    for row in range(own):
        for place in range(own):
            rows_ref[pl.ds(row * count + place, peers, stride=own)] = cells_ref[
                pl.ds(row * own + place, peers, stride=cell_rows)
            ]
    summed = recv_ref[0, cell_rows : cell_rows + own * bias_rows].astype(jnp.float32)
    for peer in range(1, peers):
        summed = summed + recv_ref[peer, cell_rows : cell_rows + own * bias_rows].astype(jnp.float32)
    bias_ref[...] = summed
    for row in range(own):
        pieces = []
        for head in range(heads):
            if count < lanes:
                each = lanes // count
                place = (head % each) * count
                line = row * bias_rows + head // each
                pieces.append(bias_ref[line : line + 1, place : place + count])
            else:
                parts = count // lanes
                line = row * bias_rows + head * parts
                pieces.append(
                    jnp.concatenate([bias_ref[line + part : line + part + 1] for part in range(parts)], axis=1)
                )
        bias_grad = half(jnp.concatenate(pieces, axis=0))
        rows = slice(row * count, (row + 1) * count)
        unit = unit_ref[rows]
        grad = (rows_ref[rows] + whole(tn(bias_grad, bias_weight_ref[...]))) * gain_ref[...]
        along = jnp.mean(grad * unit, axis=-1, keepdims=True)
        result = inverse_ref[rows] * (grad - jnp.mean(grad, axis=-1, keepdims=True) - unit * along)
        out_ref[row] = half(result)


def swap_cores(values):
    size = lax.axis_size("sub")
    return lax.ppermute(values, "sub", [(place, place ^ 1) for place in range(size)])


def exchange(values):
    return lax.all_to_all(values, group_axes, split_axis=0, concat_axis=0, tiled=True)


def local(
    pair,
    cotangent,
    residue_mask,
    chain_labels,
    gain,
    projection_weight,
    bias_weight,
    output_weight,
    position_bias_table,
    adapter_down_maps,
    adapter_up_maps,
):
    own, count, channels = pair.shape
    peers = count // own
    heads = position_bias_table.shape[0]
    rank = adapter_up_maps.shape[1]
    total = own * count
    cell_rows = own * own
    bias_rows = heads * count // lanes
    adapter_rows = 8 * rank
    adapter_chunk = adapter_rows // 4
    bias_chunk = own * bias_rows
    f32, bf16 = jnp.float32, jnp.bfloat16
    gain_row = gain.reshape(1, channels)
    bias_weight_t = bias_weight.T
    downs = jnp.swapaxes(adapter_down_maps, 1, 2)
    params = pltpu.CompilerParams(vmem_limit_bytes=(16 if total <= 1024 else 56) * 1024 * 1024)

    first_send, unit, inverse = pl.pallas_call(
        before_kernel,
        out_shape=(
            jax.ShapeDtypeStruct((peers, 2 * cell_rows + bias_chunk, channels), bf16),
            jax.ShapeDtypeStruct((total, channels), f32),
            jax.ShapeDtypeStruct((total, 1), f32),
        ),
        in_specs=[smem, smem] + [vmem] * 6,
        out_specs=(vmem, vmem, vmem),
        scratch_shapes=[
            pltpu.VMEM((total, channels), f32),
            pltpu.VMEM((total, channels), f32),
            pltpu.VMEM((bias_chunk, lanes), f32),
        ],
        compiler_params=params,
        name="before",
    )(
        residue_mask, chain_labels, chain_labels.reshape(1, count), pair, cotangent, gain_row,
        bias_weight_t, position_bias_table,
    )
    first_recv = exchange(first_send)
    cells, keep, give = pl.pallas_call(
        functools.partial(middle_kernel, own=own, heads=heads),
        out_shape=(
            jax.ShapeDtypeStruct((peers, cell_rows + bias_chunk, channels), bf16),
            jax.ShapeDtypeStruct((adapter_rows // 2, channels), f32),
            jax.ShapeDtypeStruct((adapter_rows // 2, channels), f32),
        ),
        in_specs=[vmem] * 5,
        out_specs=(vmem,) * 3,
        scratch_shapes=[
            pltpu.VMEM((total, channels), f32),
            pltpu.VMEM((total, channels), bf16),
            pltpu.VMEM((total, channels), bf16),
            pltpu.VMEM((count, heads * count), f32),
            *[pltpu.VMEM((total, channels), bf16)] * 5,
            *[pltpu.VMEM((total, channels), f32)] * 6,
            pltpu.VMEM((count * bias_rows, lanes), f32),
            pltpu.VMEM((adapter_rows, channels), f32),
            pltpu.VMEM((total, channels), f32),
        ],
        compiler_params=params,
        name="middle",
    )(first_recv, projection_weight, output_weight, downs, adapter_up_maps)
    second_send = pl.pallas_call(
        pack_kernel,
        out_shape=jax.ShapeDtypeStruct((peers, cell_rows + bias_chunk + adapter_chunk, channels), bf16),
        in_specs=[vmem] * 3,
        out_specs=vmem,
        compiler_params=params,
        name="pack",
    )(cells, keep, swap_cores(give))
    second_recv = exchange(second_send)
    mine = pl.pallas_call(
        functools.partial(adapter_kernel, offset=cell_rows + bias_chunk),
        out_shape=jax.ShapeDtypeStruct((adapter_rows // 2, channels), f32),
        in_specs=[vmem],
        out_specs=vmem,
        compiler_params=params,
        name="adapters",
    )(second_recv)
    pair_grad, down_grad, up_grad = pl.pallas_call(
        after_kernel,
        out_shape=(
            jax.ShapeDtypeStruct((own, count, channels), bf16),
            jax.ShapeDtypeStruct((adapter_rows // 2, channels), f32),
            jax.ShapeDtypeStruct((adapter_rows // 2, channels), f32),
        ),
        in_specs=[vmem] * 7,
        out_specs=(vmem,) * 3,
        scratch_shapes=[
            pltpu.VMEM((total, channels), f32),
            pltpu.VMEM((total, channels), f32),
            pltpu.VMEM((bias_chunk, lanes), f32),
        ],
        compiler_params=params,
        name="after",
    )(second_recv, mine, swap_cores(mine), unit, inverse, gain_row, bias_weight_t)
    return (
        pair_grad,
        jnp.swapaxes(down_grad.reshape(4, rank, channels), 1, 2),
        up_grad.reshape(4, rank, channels),
    )


def solution(mesh):
    return jax.shard_map(
        local,
        mesh=mesh,
        in_specs=(
            P(("groups", "dap", "sub"), None, None),
            P(("groups", "dap", "sub"), None, None),
            P("groups"),
            P("groups"),
            P(),
            P(),
            P(),
            P(),
            P(),
            P(),
            P(),
        ),
        out_specs=(
            P(("groups", "dap", "sub"), None, None),
            P("groups", None, None),
            P("groups", None, None),
        ),
        check_vma=False,
    )
```

```python
import functools
import math

import jax
import jax.numpy as jnp
from jax import lax
from jax.experimental import pallas as pl
from jax.experimental.pallas import tpu as pltpu
from jax.sharding import PartitionSpec as P

epsilon = 1e-05
lanes = 128
block = 256
masked_bias = -3e38
group_axes = ("dap", "sub")
vmem = pl.BlockSpec(memory_space=pltpu.VMEM)
hbm = pl.BlockSpec(memory_space=pltpu.HBM)


def nn(left, right):
    return jnp.dot(left, right, preferred_element_type=jnp.float32)


def nt(left, right):
    return lax.dot_general(left, right, (((1,), (1,)), ((), ())), preferred_element_type=jnp.float32)


def tn(left, right):
    return lax.dot_general(left, right, (((0,), (0,)), ((), ())), preferred_element_type=jnp.float32)


def half(values):
    return values.astype(jnp.bfloat16)


def repeat(count, body):
    if count == 1:
        body(0)
    else:
        lax.fori_loop(0, count, lambda step, carry: (body(step), carry)[1], 0)


def before_kernel(
    mask_hbm, label_hbm, label_row_hbm, pair_hbm, cot_hbm, gain_hbm, bias_weight_hbm, table_hbm,
    send_ref, unit_ref, inverse_ref, gain_ref, bias_weight_ref,
    normed_ref, cells_ref, bias_ref, mask_ref, label_ref, label_row_ref, pair_ref, cot_ref, table_ref, sems,
):
    copies = [
        pltpu.make_async_copy(source, target, sems.at[index])
        for index, (source, target) in enumerate((
            (pair_hbm, pair_ref), (mask_hbm, mask_ref), (label_hbm, label_ref), (label_row_hbm, label_row_ref),
            (gain_hbm, gain_ref), (bias_weight_hbm, bias_weight_ref), (table_hbm, table_ref), (cot_hbm, cot_ref),
        ))
    ]
    for copy in copies:
        copy.start()
    for copy in copies[:-1]:
        copy.wait()
    own, count, channels = pair_ref.shape
    peers = count // own
    heads, bins = table_ref.shape
    reach = (bins - 2) // 2
    first = lax.axis_index(group_axes) * own
    bias_rows = heads * count // lanes
    gain = gain_ref[...]
    key_pos = lax.broadcasted_iota(jnp.int32, (1, count), 1)
    bin_ids = lax.broadcasted_iota(jnp.int32, (bins, count), 0)
    for row in range(own):
        here = first + row
        values = pair_ref[row].astype(jnp.float32)
        centred = values - jnp.mean(values, axis=-1, keepdims=True)
        inverse = lax.rsqrt(jnp.mean(centred * centred, axis=-1, keepdims=True) + epsilon)
        unit = centred * inverse
        normed = unit * gain
        unit_ref[row * count : (row + 1) * count] = unit
        inverse_ref[row * count : (row + 1) * count] = inverse
        normed_ref[row * count : (row + 1) * count] = normed
        same = label_row_ref[...] == label_ref[here]
        offset = jnp.clip(here - key_pos, -reach, reach) + reach
        onehot = (bin_ids == jnp.where(same, offset, bins - 1)).astype(jnp.float32)
        relative = lax.dot_general(
            table_ref[...], onehot, (((1,), (0,)), ((), ())),
            precision=lax.Precision.HIGHEST, preferred_element_type=jnp.float32,
        )
        bias = half(nt(bias_weight_ref[...], half(normed)) + relative).astype(jnp.float32)
        bias = jnp.where(mask_ref[here] > 0, bias, masked_bias)
        for head in range(heads):
            if count < lanes:
                each = lanes // count
                place = (head % each) * count
                bias_ref[row * bias_rows + head // each, place : place + count] = bias[head]
            else:
                for part in range(count // lanes):
                    bias_ref[row * bias_rows + head * (count // lanes) + part, :] = bias[
                        head, part * lanes : (part + 1) * lanes
                    ]
    cell_rows = own * own

    def scatter():
        for row in range(own):
            for place in range(own):
                cells_ref[pl.ds(row * own + place, peers, stride=cell_rows)] = normed_ref[
                    pl.ds(row * count + place, peers, stride=own)
                ]
        return half(cells_ref[...]).reshape(peers, cell_rows, channels)

    send_ref[:, 0:cell_rows] = scatter()
    copies[-1].wait()
    for row in range(own):
        normed_ref[row * count : (row + 1) * count] = cot_ref[row].astype(jnp.float32)
    send_ref[:, cell_rows : 2 * cell_rows] = scatter()
    bias_all = half(bias_ref[...])
    send_ref[:, 2 * cell_rows :] = jnp.broadcast_to(bias_all[None], (peers, *bias_all.shape))


def middle_kernel(
    recv_ref, weight_ref, out_weight_ref, down_ref, up_ref,
    send_ref, keep_ref, give_ref,
    rows_ref, x_ref, u_ref, bias_ref, q_ref, k_ref, v_ref, da_ref, da2_ref, gate_ref, dgated_ref,
    att_ref, dq_ref, dk_ref, dv_ref, bias_grad_ref, adapter_ref, cells_ref,
    *, own, heads,
):
    peers = recv_ref.shape[0]
    channels = recv_ref.shape[2]
    count = own * peers
    cell_rows = own * own
    width = channels // heads
    scale = 1.0 / math.sqrt(width)
    rank = down_ref.shape[1]
    bias_rows = heads * count // lanes
    total = own * count
    joint = min(count, block)
    joint_heads = block // joint

    for target, offset in ((x_ref, 0), (u_ref, cell_rows)):
        rows_ref[...] = recv_ref[:, offset : offset + cell_rows].astype(jnp.float32).reshape(total, channels)
        for place in range(own):
            target[place * count : (place + 1) * count] = half(rows_ref[pl.ds(place, count, stride=own)])
    gathered = recv_ref[:, 2 * cell_rows :].astype(jnp.float32)
    bias_grad_ref[...] = gathered.reshape(count * bias_rows, lanes)
    for part in range(bias_rows):
        bias_ref[:, part * lanes : (part + 1) * lanes] = bias_grad_ref[pl.ds(part, count, stride=bias_rows)]

    weights = [weight_ref[index] for index in range(4)]
    downs = [down_ref[index] for index in range(4)]
    ups = [up_ref[index] for index in range(4)]

    def project(step):
        rows = pl.ds(pl.multiple_of(step * block, block), block)
        x = x_ref[rows]
        u = u_ref[rows]
        for index, target in enumerate((q_ref, k_ref, v_ref)):
            low = half(nt(x, downs[index]))
            target[rows] = half(nn(x, weights[index]) + nn(low, ups[index]))
        gate = jax.nn.sigmoid(nn(x, weights[3]))
        dgated = nt(u, out_weight_ref[...]) + nn(half(nt(u, ups[3])), downs[3])
        gate_ref[rows] = gate
        dgated_ref[rows] = dgated
        dattended = dgated * gate
        leading = half(dattended)
        da_ref[rows] = leading
        da2_ref[rows] = half(dattended - leading.astype(jnp.float32))

    repeat(total // block, project)

    head_of = lax.broadcasted_iota(jnp.int32, (1, channels), 1) // width
    blocks = heads * count // block

    def attend(row, part):
        start = part * block // count
        column = pl.multiple_of(part * block, block)
        first = 0 if count <= block else pl.multiple_of(lax.rem(part * block, count), block)
        queries = pl.ds(row * count + first, joint)
        keys = pl.ds(row * count, count)
        spots = [(head_of == start + head).astype(jnp.float32) for head in range(joint_heads)]

        def spread(values):
            return jnp.concatenate([values * half(spot) for spot in spots], axis=0)

        def collect(values):
            return sum(values[head * joint : (head + 1) * joint] * spots[head] for head in range(joint_heads))

        q_wide = spread(q_ref[queries])
        da_wide = spread(da_ref[queries])
        da2_wide = spread(da2_ref[queries])
        k_all = k_ref[keys]
        v_all = v_ref[keys]
        bias = bias_ref[:, pl.ds(column, block)]
        valid = bias > -1e38
        scores = jnp.where(valid, nt(k_all, q_wide) * scale + bias, -1000000000.0)
        powers = jnp.exp(scores - jnp.max(scores, axis=0, keepdims=True))
        chances = powers / jnp.sum(powers, axis=0, keepdims=True)
        rounded = half(chances)
        dchances = half(nt(v_all, da_wide) + nt(v_all, da2_wide)).astype(jnp.float32)
        inner = dchances * chances
        dscores = inner - chances * jnp.sum(inner, axis=0, keepdims=True)
        dscores = jnp.where(valid, dscores, 0.0)
        scaled = half(dscores * scale)
        rest = half(dscores * scale - scaled.astype(jnp.float32))
        return (
            queries, keys, column,
            collect(tn(rounded, v_all)), collect(tn(scaled, k_all) + tn(rest, k_all)),
            nn(scaled, q_wide) + nn(rest, q_wide), nn(rounded, da_wide) + nn(rounded, da2_wide), dscores,
        )

    if blocks == 1:
        bias_grad = None
        for row in range(own):
            queries, keys, column, att, dq, dk, dv, dscores = attend(row, 0)
            att_ref[queries] = att
            dq_ref[queries] = dq
            dk_ref[keys] = dk
            dv_ref[keys] = dv
            bias_grad = dscores if bias_grad is None else bias_grad + dscores
        bias_ref[...] = bias_grad
    else:
        bias_sum_ref = bias_grad_ref
        for ref in (att_ref, dq_ref, dk_ref, dv_ref):
            ref[...] = jnp.zeros_like(ref)

        def each(part):
            def each_row(row, bias_grad):
                queries, keys, column, att, dq, dk, dv, dscores = attend(row, part)
                att_ref[queries] += att
                dq_ref[queries] += dq
                dk_ref[keys] += dk
                dv_ref[keys] += dv
                return bias_grad + dscores

            bias_grad = lax.fori_loop(0, own, each_row, jnp.zeros((count, block), jnp.float32))
            bias_ref[:, pl.ds(pl.multiple_of(part * block, block), block)] = bias_grad

        repeat(blocks, each)
    for part in range(bias_rows):
        bias_grad_ref[pl.ds(part, count, stride=bias_rows)] = bias_ref[:, part * lanes : (part + 1) * lanes]

    adapter_ref[...] = jnp.zeros_like(adapter_ref)

    def finish(step):
        rows = pl.ds(pl.multiple_of(step * block, block), block)
        x = x_ref[rows]
        u = u_ref[rows]
        att = att_ref[rows]
        gate = gate_ref[rows]
        dgated = dgated_ref[rows]
        gated = half(gate * att)
        dgate = half(dgated * att * (gate * (1.0 - gate)))
        low_out = half(nt(downs[3], gated))
        dlow_out = half(nt(ups[3], u))
        downs_grad = [None] * 3 + [nn(dlow_out, gated)]
        ups_grad = [None] * 3 + [nn(low_out, u)]
        grad = nt(dgate, weights[3])
        for index, source in enumerate((dq_ref, dk_ref, dv_ref)):
            dproj = half(source[rows])
            ups_grad[index] = nn(half(nt(downs[index], x)), dproj)
            downs_grad[index] = nn(half(nt(ups[index], dproj)), x)
            grad = grad + nt(dproj, weights[index]) + nn(half(nt(dproj, ups[index])), downs[index])
        for index in range(4):
            adapter_ref[index * rank : (index + 1) * rank] += downs_grad[index]
            adapter_ref[(4 + index) * rank : (5 + index) * rank] += ups_grad[index]
        rows_ref[rows] = grad

    repeat(total // block, finish)

    bias_chunk = own * bias_rows
    for row in range(own):
        for place in range(own):
            cells_ref[pl.ds(row * own + place, peers, stride=cell_rows)] = rows_ref[
                pl.ds(place * count + row, peers, stride=own)
            ]
    send_ref[:, 0:cell_rows] = half(cells_ref[...]).reshape(peers, cell_rows, channels)
    send_ref[:, cell_rows:] = half(bias_grad_ref[...]).reshape(peers, bias_chunk, lanes)
    side = lax.rem(lax.axis_index("sub"), 2) == 0
    split = adapter_ref.shape[0] // 2
    keep_ref[...] = jnp.where(side, adapter_ref[:split], adapter_ref[split:])
    give_ref[...] = jnp.where(side, adapter_ref[split:], adapter_ref[:split])


def pack_kernel(cells_ref, keep_ref, taken_ref, send_ref):
    peers, rows, _ = cells_ref.shape
    send_ref[:, :rows] = cells_ref[...]
    summed = half(keep_ref[...] + taken_ref[...])
    quarter = summed.shape[0] // 2
    for peer in range(peers):
        side = peer % 2
        send_ref[peer, rows:] = summed[side * quarter : (side + 1) * quarter]


def adapter_kernel(recv_ref, out_ref, *, offset):
    quarter = out_ref.shape[0] // 2
    for side in range(2):
        total = recv_ref[side, offset:].astype(jnp.float32)
        for peer in range(side + 2, recv_ref.shape[0], 2):
            total = total + recv_ref[peer, offset:].astype(jnp.float32)
        out_ref[side * quarter : (side + 1) * quarter] = total


def after_kernel(
    recv_ref, mine_ref, theirs_ref, unit_ref, inverse_ref, gain_ref, bias_weight_ref,
    out_ref, down_ref, up_ref, rows_ref, cells_ref, bias_ref,
):
    own, count, channels = out_ref.shape
    peers = count // own
    heads = bias_weight_ref.shape[0]
    cell_rows = own * own
    bias_rows = heads * count // lanes
    side = lax.rem(lax.axis_index("sub"), 2) == 0
    quarter = mine_ref.shape[0] // 2
    for index, ref in enumerate((down_ref, up_ref)):
        mine = mine_ref[index * quarter : (index + 1) * quarter]
        theirs = theirs_ref[index * quarter : (index + 1) * quarter]
        ref[:quarter] = jnp.where(side, mine, theirs)
        ref[quarter:] = jnp.where(side, theirs, mine)
    cells_ref[...] = recv_ref[:, :cell_rows].astype(jnp.float32).reshape(own * count, channels)
    for row in range(own):
        for place in range(own):
            rows_ref[pl.ds(row * count + place, peers, stride=own)] = cells_ref[
                pl.ds(row * own + place, peers, stride=cell_rows)
            ]
    summed = recv_ref[0, cell_rows : cell_rows + own * bias_rows].astype(jnp.float32)
    for peer in range(1, peers):
        summed = summed + recv_ref[peer, cell_rows : cell_rows + own * bias_rows].astype(jnp.float32)
    bias_ref[...] = summed
    for row in range(own):
        pieces = []
        for head in range(heads):
            if count < lanes:
                each = lanes // count
                place = (head % each) * count
                line = row * bias_rows + head // each
                pieces.append(bias_ref[line : line + 1, place : place + count])
            else:
                parts = count // lanes
                line = row * bias_rows + head * parts
                pieces.append(
                    jnp.concatenate([bias_ref[line + part : line + part + 1] for part in range(parts)], axis=1)
                )
        bias_grad = half(jnp.concatenate(pieces, axis=0))
        rows = slice(row * count, (row + 1) * count)
        unit = unit_ref[rows]
        grad = (rows_ref[rows] + tn(bias_grad, bias_weight_ref[...])) * gain_ref[...]
        along = jnp.mean(grad * unit, axis=-1, keepdims=True)
        result = inverse_ref[rows] * (grad - jnp.mean(grad, axis=-1, keepdims=True) - unit * along)
        out_ref[row] = half(result)


def swap_cores(values):
    size = lax.axis_size("sub")
    return lax.ppermute(values, "sub", [(place, place ^ 1) for place in range(size)])


def exchange(values):
    return lax.all_to_all(values, group_axes, split_axis=0, concat_axis=0, tiled=True)


def local(
    pair,
    cotangent,
    residue_mask,
    chain_labels,
    gain,
    projection_weight,
    bias_weight,
    output_weight,
    position_bias_table,
    adapter_down_maps,
    adapter_up_maps,
):
    own, count, channels = pair.shape
    peers = count // own
    heads = position_bias_table.shape[0]
    rank = adapter_up_maps.shape[1]
    total = own * count
    cell_rows = own * own
    bias_rows = heads * count // lanes
    adapter_rows = 8 * rank
    adapter_chunk = adapter_rows // 4
    bias_chunk = own * bias_rows
    f32, bf16 = jnp.float32, jnp.bfloat16
    gain_row = gain.reshape(1, channels)
    bias_weight_t = bias_weight.T
    downs = jnp.swapaxes(adapter_down_maps, 1, 2)
    params = pltpu.CompilerParams(vmem_limit_bytes=(16 if total <= 1024 else 56) * 1024 * 1024)

    first_send, unit, inverse, gain_kept, bias_weight_kept = pl.pallas_call(
        before_kernel,
        out_shape=(
            jax.ShapeDtypeStruct((peers, 2 * cell_rows + bias_chunk, channels), bf16),
            jax.ShapeDtypeStruct((total, channels), f32),
            jax.ShapeDtypeStruct((total, 1), f32),
            jax.ShapeDtypeStruct((1, channels), f32),
            jax.ShapeDtypeStruct((heads, channels), bf16),
        ),
        in_specs=[hbm] * 8,
        out_specs=(vmem,) * 5,
        scratch_shapes=[
            pltpu.VMEM((total, channels), f32),
            pltpu.VMEM((total, channels), f32),
            pltpu.VMEM((bias_chunk, lanes), f32),
            pltpu.SMEM((count,), jnp.int32),
            pltpu.SMEM((count,), jnp.int32),
            pltpu.VMEM((1, count), jnp.int32),
            pltpu.VMEM(pair.shape, bf16),
            pltpu.VMEM(pair.shape, bf16),
            pltpu.VMEM(position_bias_table.shape, f32),
            pltpu.SemaphoreType.DMA((8,)),
        ],
        compiler_params=params,
        name="before",
    )(
        *(
            pltpu.with_memory_space_constraint(value, pltpu.HBM)
            for value in (
                residue_mask, chain_labels, chain_labels.reshape(1, count), pair, cotangent, gain_row,
                bias_weight_t, position_bias_table,
            )
        )
    )
    first_recv = exchange(first_send)
    cells, keep, give = pl.pallas_call(
        functools.partial(middle_kernel, own=own, heads=heads),
        out_shape=(
            jax.ShapeDtypeStruct((peers, cell_rows + bias_chunk, channels), bf16),
            jax.ShapeDtypeStruct((adapter_rows // 2, channels), f32),
            jax.ShapeDtypeStruct((adapter_rows // 2, channels), f32),
        ),
        in_specs=[vmem] * 5,
        out_specs=(vmem,) * 3,
        scratch_shapes=[
            pltpu.VMEM((total, channels), f32),
            pltpu.VMEM((total, channels), bf16),
            pltpu.VMEM((total, channels), bf16),
            pltpu.VMEM((count, heads * count), f32),
            *[pltpu.VMEM((total, channels), bf16)] * 5,
            *[pltpu.VMEM((total, channels), f32)] * 6,
            pltpu.VMEM((count * bias_rows, lanes), f32),
            pltpu.VMEM((adapter_rows, channels), f32),
            pltpu.VMEM((total, channels), f32),
        ],
        compiler_params=params,
        name="middle",
    )(first_recv, projection_weight, output_weight, downs, adapter_up_maps)
    second_send = pl.pallas_call(
        pack_kernel,
        out_shape=jax.ShapeDtypeStruct((peers, cell_rows + bias_chunk + adapter_chunk, channels), bf16),
        in_specs=[vmem] * 3,
        out_specs=vmem,
        compiler_params=params,
        name="pack",
    )(cells, keep, swap_cores(give))
    second_recv = exchange(second_send)
    mine = pl.pallas_call(
        functools.partial(adapter_kernel, offset=cell_rows + bias_chunk),
        out_shape=jax.ShapeDtypeStruct((adapter_rows // 2, channels), f32),
        in_specs=[vmem],
        out_specs=vmem,
        compiler_params=params,
        name="adapters",
    )(second_recv)
    pair_grad, down_grad, up_grad = pl.pallas_call(
        after_kernel,
        out_shape=(
            jax.ShapeDtypeStruct((own, count, channels), bf16),
            jax.ShapeDtypeStruct((adapter_rows // 2, channels), f32),
            jax.ShapeDtypeStruct((adapter_rows // 2, channels), f32),
        ),
        in_specs=[vmem] * 7,
        out_specs=(vmem,) * 3,
        scratch_shapes=[
            pltpu.VMEM((total, channels), f32),
            pltpu.VMEM((total, channels), f32),
            pltpu.VMEM((bias_chunk, lanes), f32),
        ],
        compiler_params=params,
        name="after",
    )(second_recv, mine, swap_cores(mine), unit, inverse, gain_kept, bias_weight_kept)
    return (
        pair_grad,
        jnp.swapaxes(down_grad.reshape(4, rank, channels), 1, 2),
        up_grad.reshape(4, rank, channels),
    )


def solution(mesh):
    return jax.shard_map(
        local,
        mesh=mesh,
        in_specs=(
            P(("groups", "dap", "sub"), None, None),
            P(("groups", "dap", "sub"), None, None),
            P("groups"),
            P("groups"),
            P(),
            P(),
            P(),
            P(),
            P(),
            P(),
            P(),
        ),
        out_specs=(
            P(("groups", "dap", "sub"), None, None),
            P("groups", None, None),
            P("groups", None, None),
        ),
        check_vma=False,
    )
```

```python
import functools
import math

import jax
import jax.numpy as jnp
from jax import lax
from jax.experimental import pallas as pl
from jax.experimental.pallas import tpu as pltpu
from jax.sharding import PartitionSpec as P

epsilon = 1e-05
lanes = 128
block = 256
masked_bias = -3e38
group_axes = ("dap", "sub")
vmem = pl.BlockSpec(memory_space=pltpu.VMEM)
hbm = pl.BlockSpec(memory_space=pltpu.HBM)


def nn(left, right):
    return jnp.dot(left, right, preferred_element_type=jnp.float32)


def nt(left, right):
    return lax.dot_general(left, right, (((1,), (1,)), ((), ())), preferred_element_type=jnp.float32)


def tn(left, right):
    return lax.dot_general(left, right, (((0,), (0,)), ((), ())), preferred_element_type=jnp.float32)


def half(values):
    return values.astype(jnp.bfloat16)


def repeat(count, body):
    if count == 1:
        body(0)
    else:
        lax.fori_loop(0, count, lambda step, carry: (body(step), carry)[1], 0)


def before_kernel(
    mask_hbm, label_hbm, label_row_hbm, pair_hbm, cot_hbm, gain_hbm, bias_weight_hbm, table_hbm,
    send_ref, unit_ref, inverse_ref, gain_ref, bias_weight_ref,
    normed_ref, cells_ref, bias_ref, mask_ref, label_ref, label_row_ref, pair_ref, cot_ref, table_ref, sems,
):
    copies = [
        pltpu.make_async_copy(source, target, sems.at[index])
        for index, (source, target) in enumerate((
            (pair_hbm, pair_ref), (mask_hbm, mask_ref), (label_hbm, label_ref), (label_row_hbm, label_row_ref),
            (gain_hbm, gain_ref), (bias_weight_hbm, bias_weight_ref), (table_hbm, table_ref), (cot_hbm, cot_ref),
        ))
    ]
    for copy in copies:
        copy.start()
    for copy in copies[:-1]:
        copy.wait()
    own, count, channels = pair_ref.shape
    peers = count // own
    heads, bins = table_ref.shape
    reach = (bins - 2) // 2
    first = lax.axis_index(group_axes) * own
    bias_rows = heads * count // lanes
    gain = gain_ref[...]
    key_pos = lax.broadcasted_iota(jnp.int32, (1, count), 1)
    bin_ids = lax.broadcasted_iota(jnp.int32, (bins, count), 0)
    for row in range(own):
        here = first + row
        values = pair_ref[row].astype(jnp.float32)
        centred = values - jnp.mean(values, axis=-1, keepdims=True)
        inverse = lax.rsqrt(jnp.mean(centred * centred, axis=-1, keepdims=True) + epsilon)
        unit = centred * inverse
        normed = unit * gain
        unit_ref[row * count : (row + 1) * count] = unit
        inverse_ref[row * count : (row + 1) * count] = inverse
        normed_ref[row * count : (row + 1) * count] = normed
        same = label_row_ref[...] == label_ref[here]
        offset = jnp.clip(here - key_pos, -reach, reach) + reach
        onehot = (bin_ids == jnp.where(same, offset, bins - 1)).astype(jnp.float32)
        relative = lax.dot_general(
            table_ref[...], onehot, (((1,), (0,)), ((), ())),
            precision=lax.Precision.HIGHEST, preferred_element_type=jnp.float32,
        )
        bias = half(nt(bias_weight_ref[...], half(normed)) + relative).astype(jnp.float32)
        bias = jnp.where(mask_ref[here] > 0, bias, masked_bias)
        for head in range(heads):
            if count < lanes:
                each = lanes // count
                place = (head % each) * count
                bias_ref[row * bias_rows + head // each, place : place + count] = bias[head]
            else:
                for part in range(count // lanes):
                    bias_ref[row * bias_rows + head * (count // lanes) + part, :] = bias[
                        head, part * lanes : (part + 1) * lanes
                    ]
    cell_rows = own * own

    def scatter():
        for row in range(own):
            for place in range(own):
                cells_ref[pl.ds(row * own + place, peers, stride=cell_rows)] = normed_ref[
                    pl.ds(row * count + place, peers, stride=own)
                ]
        return half(cells_ref[...]).reshape(peers, cell_rows, channels)

    send_ref[:, 0:cell_rows] = scatter()
    copies[-1].wait()
    for row in range(own):
        normed_ref[row * count : (row + 1) * count] = cot_ref[row].astype(jnp.float32)
    send_ref[:, cell_rows : 2 * cell_rows] = scatter()
    bias_all = half(bias_ref[...])
    send_ref[:, 2 * cell_rows :] = jnp.broadcast_to(bias_all[None], (peers, *bias_all.shape))


def stacked(maps_ref, count):
    return jnp.concatenate([maps_ref[index] for index in range(count)], axis=0)


def blocked(maps_ref, count):
    empty = jnp.zeros_like(maps_ref[0])
    return jnp.concatenate(
        [
            jnp.concatenate([maps_ref[index] if place == index else empty for place in range(count)], axis=1)
            for index in range(count)
        ],
        axis=0,
    )


def beside(weight_ref, first):
    return jnp.concatenate([weight_ref[first], weight_ref[first + 1]], axis=1)


def middle_kernel(
    recv_ref, weight_ref, out_weight_ref, down_ref, up_ref,
    dall_ref, bias_ref, keep_ref, give_ref,
    rows_ref, x_ref, u_ref, q_ref, k_ref, v_ref, da_ref, da2_ref, gate_ref, dgated_ref,
    att_ref, dq_ref, dk_ref, dv_ref, gathered_ref, adapter_ref,
    *, own, heads,
):
    peers = recv_ref.shape[0]
    channels = recv_ref.shape[2]
    count = own * peers
    cell_rows = own * own
    width = channels // heads
    scale = 1.0 / math.sqrt(width)
    rank = down_ref.shape[1]
    bias_rows = heads * count // lanes
    total = own * count
    joint = min(count, block)
    joint_heads = block // joint

    for target, offset in ((x_ref, 0), (u_ref, cell_rows)):
        rows_ref[...] = recv_ref[:, offset : offset + cell_rows].astype(jnp.float32).reshape(total, channels)
        for place in range(own):
            target[place * count : (place + 1) * count] = half(rows_ref[pl.ds(place, count, stride=own)])
    gathered = recv_ref[:, 2 * cell_rows :].astype(jnp.float32)
    gathered_ref[...] = gathered.reshape(count * bias_rows, lanes)
    for part in range(bias_rows):
        bias_ref[:, part * lanes : (part + 1) * lanes] = gathered_ref[pl.ds(part, count, stride=bias_rows)]

    downs = stacked(down_ref, 3)
    ups = blocked(up_ref, 3)

    def project(step):
        rows = pl.ds(pl.multiple_of(step * block, block), block)
        x = x_ref[rows]
        u = u_ref[rows]
        update = nn(half(nt(x, downs)), ups)
        pair01 = nn(x, beside(weight_ref, 0))
        pair23 = nn(x, beside(weight_ref, 2))
        q_ref[rows] = half(pair01[:, :channels] + update[:, :channels])
        k_ref[rows] = half(pair01[:, channels:] + update[:, channels : 2 * channels])
        v_ref[rows] = half(pair23[:, :channels] + update[:, 2 * channels :])
        gate = jax.nn.sigmoid(pair23[:, channels:])
        dgated = nt(u, out_weight_ref[...]) + nn(half(nt(u, up_ref[3])), down_ref[3])
        gate_ref[rows] = gate
        dgated_ref[rows] = dgated
        dattended = dgated * gate
        leading = half(dattended)
        da_ref[rows] = leading
        da2_ref[rows] = half(dattended - leading.astype(jnp.float32))

    repeat(total // block, project)

    head_of = lax.broadcasted_iota(jnp.int32, (1, channels), 1) // width
    blocks = heads * count // block

    def attend(row, part):
        start = part * block // count
        column = pl.multiple_of(part * block, block)
        first = 0 if count <= block else pl.multiple_of(lax.rem(part * block, count), block)
        queries = pl.ds(row * count + first, joint)
        keys = pl.ds(row * count, count)
        spots = [(head_of == start + head).astype(jnp.float32) for head in range(joint_heads)]

        def spread(values):
            return jnp.concatenate([values * half(spot) for spot in spots], axis=0)

        def collect(values):
            return sum(values[head * joint : (head + 1) * joint] * spots[head] for head in range(joint_heads))

        q_wide = spread(q_ref[queries])
        da_wide = jnp.concatenate([spread(da_ref[queries]), spread(da2_ref[queries])], axis=1)
        k_all = k_ref[keys]
        v_all = v_ref[keys]
        bias = bias_ref[:, pl.ds(column, block)]
        valid = bias > -1e38
        scores = jnp.where(valid, nt(k_all, q_wide) * scale + bias, -1000000000.0)
        powers = jnp.exp(scores - jnp.max(scores, axis=0, keepdims=True))
        chances = powers * (1.0 / jnp.sum(powers, axis=0, keepdims=True))
        rounded = half(chances)
        dchances = half(nt(jnp.concatenate([v_all, v_all], axis=1), da_wide)).astype(jnp.float32)
        inner = dchances * chances
        dscores = inner - chances * jnp.sum(inner, axis=0, keepdims=True)
        dscores = jnp.where(valid, dscores, 0.0)
        scaled = dscores * scale
        leading = half(scaled)
        both = jnp.concatenate([leading, half(scaled - leading.astype(jnp.float32))], axis=0)
        dk = nn(both, q_wide)
        dv = nn(rounded, da_wide)
        return (
            queries, keys,
            collect(tn(rounded, v_all)), collect(tn(both, jnp.concatenate([k_all, k_all], axis=0))),
            dk[:count] + dk[count:], dv[:, :channels] + dv[:, channels:], dscores,
        )

    if blocks == 1:
        bias_grad = None
        for row in range(own):
            queries, keys, att, dq, dk, dv, dscores = attend(row, 0)
            att_ref[queries] = att
            dq_ref[queries] = dq
            dk_ref[keys] = dk
            dv_ref[keys] = dv
            bias_grad = dscores if bias_grad is None else bias_grad + dscores
        bias_ref[...] = bias_grad
    else:
        for ref in (att_ref, dq_ref, dk_ref, dv_ref):
            ref[...] = jnp.zeros_like(ref)

        def each(part):
            def each_row(row, bias_grad):
                queries, keys, att, dq, dk, dv, dscores = attend(row, part)
                att_ref[queries] += att
                dq_ref[queries] += dq
                dk_ref[keys] += dk
                dv_ref[keys] += dv
                return bias_grad + dscores

            bias_grad = lax.fori_loop(0, own, each_row, jnp.zeros((count, block), jnp.float32))
            bias_ref[:, pl.ds(pl.multiple_of(part * block, block), block)] = bias_grad

        repeat(blocks, each)

    many = total > block
    if many:
        adapter_ref[...] = jnp.zeros_like(adapter_ref)

    def finish(step):
        rows = pl.ds(pl.multiple_of(step * block, block), block)
        x = x_ref[rows]
        u = u_ref[rows]
        att = att_ref[rows]
        gate = gate_ref[rows]
        gated = half(gate * att)
        dgate = half(dgated_ref[rows] * att * (gate * (1.0 - gate)))
        dproj = [half(ref[rows]) for ref in (dq_ref, dk_ref, dv_ref)]
        dprojs = jnp.concatenate(dproj, axis=1)
        dall_ref[rows, : 3 * channels] = dprojs
        dall_ref[rows, 3 * channels :] = dgate
        low = half(nt(downs, x))
        dlow = half(nt(ups, dprojs))
        grads = [
            nn(dlow, x),
            nn(half(nt(up_ref[3], u)), gated),
            *[nn(low[index * rank : (index + 1) * rank], dproj[index]) for index in range(3)],
            nn(half(nt(down_ref[3], gated)), u),
        ]
        grads = jnp.concatenate(grads, axis=0)
        adapter_ref[...] = adapter_ref[...] + grads if many else grads

    repeat(total // block, finish)

    side = lax.rem(lax.axis_index("sub"), 2) == 0
    split = adapter_ref.shape[0] // 2
    keep_ref[...] = jnp.where(side, adapter_ref[:split], adapter_ref[split:])
    give_ref[...] = jnp.where(side, adapter_ref[split:], adapter_ref[:split])


def cells_kernel(
    dall_ref, bias_ref, weight_ref, down_ref, up_ref, send_ref, rows_ref, cells_ref, bias_rows_ref, *, own
):
    peers = send_ref.shape[0]
    channels = send_ref.shape[2]
    count = own * peers
    cell_rows = own * own
    total = own * count
    bias_rows = bias_ref.shape[1] // lanes
    downs = stacked(down_ref, 3)
    ups = blocked(up_ref, 3)

    def rows_of(step):
        rows = pl.ds(pl.multiple_of(step * block, block), block)
        rows_ref[rows] = (
            nt(dall_ref[rows, : 2 * channels], beside(weight_ref, 0))
            + nt(dall_ref[rows, 2 * channels :], beside(weight_ref, 2))
            + nn(half(nt(dall_ref[rows, : 3 * channels], ups)), downs)
        )

    repeat(total // block, rows_of)
    for row in range(own):
        for place in range(own):
            cells_ref[pl.ds(row * own + place, peers, stride=cell_rows)] = rows_ref[
                pl.ds(place * count + row, peers, stride=own)
            ]
    for part in range(bias_rows):
        bias_rows_ref[pl.ds(part, count, stride=bias_rows)] = bias_ref[:, part * lanes : (part + 1) * lanes]
    send_ref[:, 0:cell_rows] = half(cells_ref[...]).reshape(peers, cell_rows, channels)
    send_ref[:, cell_rows:] = half(bias_rows_ref[...]).reshape(peers, own * bias_rows, lanes)


def pack_kernel(cells_ref, keep_ref, taken_ref, send_ref):
    peers, rows, _ = cells_ref.shape
    send_ref[:, :rows] = cells_ref[...]
    summed = half(keep_ref[...] + taken_ref[...])
    quarter = summed.shape[0] // 2
    for peer in range(peers):
        side = peer % 2
        send_ref[peer, rows:] = summed[side * quarter : (side + 1) * quarter]


def adapter_kernel(recv_ref, out_ref, *, offset):
    quarter = out_ref.shape[0] // 2
    for side in range(2):
        total = recv_ref[side, offset:].astype(jnp.float32)
        for peer in range(side + 2, recv_ref.shape[0], 2):
            total = total + recv_ref[peer, offset:].astype(jnp.float32)
        out_ref[side * quarter : (side + 1) * quarter] = total


def final_kernel(mine_ref, theirs_ref, down_ref, up_ref):
    side = lax.rem(lax.axis_index("sub"), 2) == 0
    quarter = mine_ref.shape[0] // 2
    for index, ref in enumerate((down_ref, up_ref)):
        mine = mine_ref[index * quarter : (index + 1) * quarter]
        theirs = theirs_ref[index * quarter : (index + 1) * quarter]
        ref[:quarter] = jnp.where(side, mine, theirs)
        ref[quarter:] = jnp.where(side, theirs, mine)


def after_kernel(
    recv_ref, unit_ref, inverse_ref, gain_ref, bias_weight_ref, out_ref, rows_ref, cells_ref, bias_ref
):
    own, count, channels = out_ref.shape
    peers = count // own
    heads = bias_weight_ref.shape[0]
    cell_rows = own * own
    bias_rows = heads * count // lanes
    cells_ref[...] = recv_ref[:, :cell_rows].astype(jnp.float32).reshape(own * count, channels)
    for row in range(own):
        for place in range(own):
            rows_ref[pl.ds(row * count + place, peers, stride=own)] = cells_ref[
                pl.ds(row * own + place, peers, stride=cell_rows)
            ]
    summed = recv_ref[0, cell_rows : cell_rows + own * bias_rows].astype(jnp.float32)
    for peer in range(1, peers):
        summed = summed + recv_ref[peer, cell_rows : cell_rows + own * bias_rows].astype(jnp.float32)
    bias_ref[...] = summed
    for row in range(own):
        pieces = []
        for head in range(heads):
            if count < lanes:
                each = lanes // count
                place = (head % each) * count
                line = row * bias_rows + head // each
                pieces.append(bias_ref[line : line + 1, place : place + count])
            else:
                parts = count // lanes
                line = row * bias_rows + head * parts
                pieces.append(
                    jnp.concatenate([bias_ref[line + part : line + part + 1] for part in range(parts)], axis=1)
                )
        bias_grad = half(jnp.concatenate(pieces, axis=0))
        rows = slice(row * count, (row + 1) * count)
        unit = unit_ref[rows]
        grad = (rows_ref[rows] + tn(bias_grad, bias_weight_ref[...])) * gain_ref[...]
        along = jnp.mean(grad * unit, axis=-1, keepdims=True)
        result = inverse_ref[rows] * (grad - jnp.mean(grad, axis=-1, keepdims=True) - unit * along)
        out_ref[row] = half(result)


def swap_cores(values):
    size = lax.axis_size("sub")
    return lax.ppermute(values, "sub", [(place, place ^ 1) for place in range(size)])


def exchange(values):
    return lax.all_to_all(values, group_axes, split_axis=0, concat_axis=0, tiled=True)


def local(
    pair,
    cotangent,
    residue_mask,
    chain_labels,
    gain,
    projection_weight,
    bias_weight,
    output_weight,
    position_bias_table,
    adapter_down_maps,
    adapter_up_maps,
):
    own, count, channels = pair.shape
    peers = count // own
    heads = position_bias_table.shape[0]
    rank = adapter_up_maps.shape[1]
    total = own * count
    cell_rows = own * own
    bias_rows = heads * count // lanes
    adapter_rows = 8 * rank
    adapter_chunk = adapter_rows // 4
    bias_chunk = own * bias_rows
    f32, bf16 = jnp.float32, jnp.bfloat16
    gain_row = gain.reshape(1, channels)
    bias_weight_t = bias_weight.T
    downs = jnp.swapaxes(adapter_down_maps, 1, 2)
    params = pltpu.CompilerParams(vmem_limit_bytes=(16 if total <= 1024 else 56) * 1024 * 1024)

    first_send, unit, inverse, gain_kept, bias_weight_kept = pl.pallas_call(
        before_kernel,
        out_shape=(
            jax.ShapeDtypeStruct((peers, 2 * cell_rows + bias_chunk, channels), bf16),
            jax.ShapeDtypeStruct((total, channels), f32),
            jax.ShapeDtypeStruct((total, 1), f32),
            jax.ShapeDtypeStruct((1, channels), f32),
            jax.ShapeDtypeStruct((heads, channels), bf16),
        ),
        in_specs=[hbm] * 8,
        out_specs=(vmem,) * 5,
        scratch_shapes=[
            pltpu.VMEM((total, channels), f32),
            pltpu.VMEM((total, channels), f32),
            pltpu.VMEM((bias_chunk, lanes), f32),
            pltpu.SMEM((count,), jnp.int32),
            pltpu.SMEM((count,), jnp.int32),
            pltpu.VMEM((1, count), jnp.int32),
            pltpu.VMEM(pair.shape, bf16),
            pltpu.VMEM(pair.shape, bf16),
            pltpu.VMEM(position_bias_table.shape, f32),
            pltpu.SemaphoreType.DMA((8,)),
        ],
        compiler_params=params,
        name="before",
    )(
        *(
            pltpu.with_memory_space_constraint(value, pltpu.HBM)
            for value in (
                residue_mask, chain_labels, chain_labels.reshape(1, count), pair, cotangent, gain_row,
                bias_weight_t, position_bias_table,
            )
        )
    )
    first_recv = exchange(first_send)
    dall, bias_grad, keep, give = pl.pallas_call(
        functools.partial(middle_kernel, own=own, heads=heads),
        out_shape=(
            jax.ShapeDtypeStruct((total, 4 * channels), bf16),
            jax.ShapeDtypeStruct((count, heads * count), f32),
            jax.ShapeDtypeStruct((adapter_rows // 2, channels), f32),
            jax.ShapeDtypeStruct((adapter_rows // 2, channels), f32),
        ),
        in_specs=[vmem] * 5,
        out_specs=(vmem,) * 4,
        scratch_shapes=[
            pltpu.VMEM((total, channels), f32),
            *[pltpu.VMEM((total, channels), bf16)] * 7,
            *[pltpu.VMEM((total, channels), f32)] * 6,
            pltpu.VMEM((count * bias_rows, lanes), f32),
            pltpu.VMEM((adapter_rows, channels), f32),
        ],
        compiler_params=params,
        name="middle",
    )(first_recv, projection_weight, output_weight, downs, adapter_up_maps)
    taken = swap_cores(give)
    cells = pl.pallas_call(
        functools.partial(cells_kernel, own=own),
        out_shape=jax.ShapeDtypeStruct((peers, cell_rows + bias_chunk, channels), bf16),
        in_specs=[vmem] * 5,
        out_specs=vmem,
        scratch_shapes=[
            pltpu.VMEM((total, channels), f32),
            pltpu.VMEM((total, channels), f32),
            pltpu.VMEM((count * bias_rows, lanes), f32),
        ],
        compiler_params=params,
        cost_estimate=pl.CostEstimate(
            flops=10 * total * channels * channels, bytes_accessed=40 * total * channels, transcendentals=0
        ),
        name="cells",
    )(dall, bias_grad, projection_weight, downs, adapter_up_maps)
    second_send = pl.pallas_call(
        pack_kernel,
        out_shape=jax.ShapeDtypeStruct((peers, cell_rows + bias_chunk + adapter_chunk, channels), bf16),
        in_specs=[vmem] * 3,
        out_specs=vmem,
        compiler_params=params,
        name="pack",
    )(cells, keep, taken)
    second_recv = exchange(second_send)
    mine = pl.pallas_call(
        functools.partial(adapter_kernel, offset=cell_rows + bias_chunk),
        out_shape=jax.ShapeDtypeStruct((adapter_rows // 2, channels), f32),
        in_specs=[vmem],
        out_specs=vmem,
        compiler_params=params,
        name="adapters",
    )(second_recv)
    theirs = swap_cores(mine)
    pair_grad = pl.pallas_call(
        after_kernel,
        out_shape=jax.ShapeDtypeStruct((own, count, channels), bf16),
        in_specs=[vmem] * 5,
        out_specs=vmem,
        scratch_shapes=[
            pltpu.VMEM((total, channels), f32),
            pltpu.VMEM((total, channels), f32),
            pltpu.VMEM((bias_chunk, lanes), f32),
        ],
        compiler_params=params,
        cost_estimate=pl.CostEstimate(
            flops=20 * total * channels, bytes_accessed=20 * total * channels, transcendentals=0
        ),
        name="after",
    )(second_recv, unit, inverse, gain_kept, bias_weight_kept)
    down_grad, up_grad = pl.pallas_call(
        final_kernel,
        out_shape=(jax.ShapeDtypeStruct((adapter_rows // 2, channels), f32),) * 2,
        in_specs=[vmem] * 2,
        out_specs=(vmem,) * 2,
        compiler_params=params,
        name="final",
    )(mine, theirs)
    return (
        pair_grad,
        jnp.swapaxes(down_grad.reshape(4, rank, channels), 1, 2),
        up_grad.reshape(4, rank, channels),
    )


def solution(mesh):
    return jax.shard_map(
        local,
        mesh=mesh,
        in_specs=(
            P(("groups", "dap", "sub"), None, None),
            P(("groups", "dap", "sub"), None, None),
            P("groups"),
            P("groups"),
            P(),
            P(),
            P(),
            P(),
            P(),
            P(),
            P(),
        ),
        out_specs=(
            P(("groups", "dap", "sub"), None, None),
            P("groups", None, None),
            P("groups", None, None),
        ),
        check_vma=False,
    )
```

```python
import functools
import math

import jax
import jax.numpy as jnp
from jax import lax
from jax.experimental import pallas as pl
from jax.experimental.pallas import tpu as pltpu
from jax.sharding import PartitionSpec as P

epsilon = 1e-05
lanes = 128
block = 256
masked_bias = -3e38
together = 4
group_axes = ("dap", "sub")
vmem = pl.BlockSpec(memory_space=pltpu.VMEM)
hbm = pl.BlockSpec(memory_space=pltpu.HBM)


def nn(left, right):
    return jnp.dot(left, right, preferred_element_type=jnp.float32)


def nt(left, right):
    return lax.dot_general(left, right, (((1,), (1,)), ((), ())), preferred_element_type=jnp.float32)


def tn(left, right):
    return lax.dot_general(left, right, (((0,), (0,)), ((), ())), preferred_element_type=jnp.float32)


def half(values):
    return values.astype(jnp.bfloat16)


def repeat(count, body):
    if count == 1:
        body(0)
    else:
        lax.fori_loop(0, count, lambda step, carry: (body(step), carry)[1], 0)


def before_kernel(
    mask_hbm, label_hbm, label_row_hbm, pair_hbm, cot_hbm, gain_hbm, bias_weight_hbm, table_hbm,
    send_ref, unit_ref, inverse_ref, gain_ref, bias_weight_ref,
    normed_ref, cells_ref, bias_ref, mask_ref, label_ref, label_row_ref, pair_ref, cot_ref, table_ref, sems,
):
    copies = [
        pltpu.make_async_copy(source, target, sems.at[index])
        for index, (source, target) in enumerate((
            (pair_hbm, pair_ref), (mask_hbm, mask_ref), (label_hbm, label_ref), (label_row_hbm, label_row_ref),
            (gain_hbm, gain_ref), (bias_weight_hbm, bias_weight_ref), (table_hbm, table_ref), (cot_hbm, cot_ref),
        ))
    ]
    for copy in copies:
        copy.start()
    for copy in copies[1:-1]:
        copy.wait()
    own, count, channels = pair_ref.shape
    peers = count // own
    heads, bins = table_ref.shape
    reach = (bins - 2) // 2
    first = lax.axis_index(group_axes) * own
    bias_rows = heads * count // lanes
    gain = gain_ref[...]
    key_pos = lax.broadcasted_iota(jnp.int32, (1, count), 1)
    bin_ids = lax.broadcasted_iota(jnp.int32, (bins, count), 0)
    table = table_ref[...]
    table_parts = []
    for _ in range(3):
        table_parts.append(half(table))
        table = table - table_parts[-1].astype(jnp.float32)
    table_parts = jnp.concatenate(table_parts, axis=0)

    def relative_bias(here):
        same = label_row_ref[...] == label_ref[here]
        offset = jnp.clip(here - key_pos, -reach, reach) + reach
        onehot = half((bin_ids == jnp.where(same, offset, bins - 1)).astype(jnp.float32))
        found = nn(table_parts, onehot)
        return found[:heads] + found[heads : 2 * heads] + found[2 * heads :]

    relative = [relative_bias(first + row) for row in range(own)]
    copies[0].wait()
    for row in range(own):
        here = first + row
        values = pair_ref[row].astype(jnp.float32)
        centred = values - jnp.mean(values, axis=-1, keepdims=True)
        inverse = lax.rsqrt(jnp.mean(centred * centred, axis=-1, keepdims=True) + epsilon)
        unit = centred * inverse
        normed = unit * gain
        unit_ref[row * count : (row + 1) * count] = unit
        inverse_ref[row * count : (row + 1) * count] = inverse
        normed_ref[row * count : (row + 1) * count] = normed
        bias = half(nt(bias_weight_ref[...], half(normed)) + relative[row]).astype(jnp.float32)
        bias = jnp.where(mask_ref[here] > 0, bias, masked_bias)
        for head in range(heads):
            if count < lanes:
                each = lanes // count
                place = (head % each) * count
                bias_ref[row * bias_rows + head // each, place : place + count] = bias[head]
            else:
                for part in range(count // lanes):
                    bias_ref[row * bias_rows + head * (count // lanes) + part, :] = bias[
                        head, part * lanes : (part + 1) * lanes
                    ]
    cell_rows = own * own

    def scatter():
        for row in range(own):
            for place in range(own):
                cells_ref[pl.ds(row * own + place, peers, stride=cell_rows)] = normed_ref[
                    pl.ds(row * count + place, peers, stride=own)
                ]
        return half(cells_ref[...]).reshape(peers, cell_rows, channels)

    send_ref[:, 0:cell_rows] = scatter()
    copies[-1].wait()
    for row in range(own):
        normed_ref[row * count : (row + 1) * count] = cot_ref[row].astype(jnp.float32)
    send_ref[:, cell_rows : 2 * cell_rows] = scatter()
    bias_all = half(bias_ref[...])
    send_ref[:, 2 * cell_rows :] = jnp.broadcast_to(bias_all[None], (peers, *bias_all.shape))


def stacked(maps_ref, count):
    return jnp.concatenate([maps_ref[index] for index in range(count)], axis=0)


def blocked(maps_ref, count):
    empty = jnp.zeros_like(maps_ref[0])
    return jnp.concatenate(
        [
            jnp.concatenate([maps_ref[index] if place == index else empty for place in range(count)], axis=1)
            for index in range(count)
        ],
        axis=0,
    )


def beside(weight_ref, first):
    return jnp.concatenate([weight_ref[first], weight_ref[first + 1]], axis=1)


def middle_kernel(
    recv_ref, weight_ref, out_weight_ref, down_ref, up_ref,
    dall_ref, bias_ref, keep_ref, give_ref,
    rows_ref, x_ref, u_ref, q_ref, k_ref, v_ref, da_ref, da2_ref, gate_ref, dgated_ref,
    att_ref, dq_ref, dk_ref, dv_ref, gathered_ref, adapter_ref,
    *, own, heads,
):
    peers = recv_ref.shape[0]
    channels = recv_ref.shape[2]
    count = own * peers
    cell_rows = own * own
    width = channels // heads
    scale = 1.0 / math.sqrt(width)
    rank = down_ref.shape[1]
    bias_rows = heads * count // lanes
    total = own * count
    joint = min(count, block)
    joint_heads = block // joint

    for target, offset in ((x_ref, 0), (u_ref, cell_rows)):
        rows_ref[...] = recv_ref[:, offset : offset + cell_rows].astype(jnp.float32).reshape(total, channels)
        for place in range(own):
            target[place * count : (place + 1) * count] = half(rows_ref[pl.ds(place, count, stride=own)])
    gathered = recv_ref[:, 2 * cell_rows :].astype(jnp.float32)
    gathered_ref[...] = gathered.reshape(count * bias_rows, lanes)
    for part in range(bias_rows):
        bias_ref[:, part * lanes : (part + 1) * lanes] = gathered_ref[pl.ds(part, count, stride=bias_rows)]

    downs = stacked(down_ref, 3)
    ups = blocked(up_ref, 3)

    def project(step):
        rows = pl.ds(pl.multiple_of(step * block, block), block)
        x = x_ref[rows]
        u = u_ref[rows]
        update = nn(half(nt(x, downs)), ups)
        pair01 = nn(x, beside(weight_ref, 0))
        pair23 = nn(x, beside(weight_ref, 2))
        q_ref[rows] = half(pair01[:, :channels] + update[:, :channels])
        k_ref[rows] = half(pair01[:, channels:] + update[:, channels : 2 * channels])
        v_ref[rows] = half(pair23[:, :channels] + update[:, 2 * channels :])
        gate = jax.nn.sigmoid(pair23[:, channels:])
        dgated = nt(u, out_weight_ref[...]) + nn(half(nt(u, up_ref[3])), down_ref[3])
        gate_ref[rows] = gate
        dgated_ref[rows] = dgated
        dattended = dgated * gate
        leading = half(dattended)
        da_ref[rows] = leading
        da2_ref[rows] = half(dattended - leading.astype(jnp.float32))

    repeat(total // block, project)

    head_of = lax.broadcasted_iota(jnp.int32, (1, channels), 1) // width
    blocks = heads * count // block

    def attend(rows, part):
        start = part * block // count
        column = pl.multiple_of(part * block, block)
        first = 0 if count <= block else pl.multiple_of(lax.rem(part * block, count), block)
        queries = [pl.ds(row * count + first, joint) for row in rows]
        keys = [pl.ds(row * count, count) for row in rows]
        spots = [(head_of == start + head).astype(jnp.float32) for head in range(joint_heads)]
        marks = [half(spot) for spot in spots]

        def spread(values):
            return jnp.concatenate([values * mark for mark in marks], axis=0)

        def collect(values):
            return sum(values[head * joint : (head + 1) * joint] * spots[head] for head in range(joint_heads))

        bias = bias_ref[:, pl.ds(column, block)]
        valid = bias > -1e38
        q_wide = [spread(q_ref[at]) for at in queries]
        da_wide = [jnp.concatenate([spread(da_ref[at]), spread(da2_ref[at])], axis=1) for at in queries]
        k_all = [k_ref[at] for at in keys]
        v_all = [v_ref[at] for at in keys]
        scores = [
            jnp.where(valid, nt(key, query) * scale + bias, -1000000000.0) for key, query in zip(k_all, q_wide)
        ]
        dchances = [
            half(nt(jnp.concatenate([value, value], axis=1), da)).astype(jnp.float32)
            for value, da in zip(v_all, da_wide)
        ]
        powers = [jnp.exp(each - jnp.max(each, axis=0, keepdims=True)) for each in scores]
        chances = [each * (1.0 / jnp.sum(each, axis=0, keepdims=True)) for each in powers]
        rounded = [half(each) for each in chances]
        att = [collect(tn(each, value)) for each, value in zip(rounded, v_all)]
        dv = [nn(each, da) for each, da in zip(rounded, da_wide)]
        inner = [left * right for left, right in zip(dchances, chances)]
        dscores = [
            jnp.where(valid, left - right * jnp.sum(left, axis=0, keepdims=True), 0.0)
            for left, right in zip(inner, chances)
        ]
        scaled = [each * scale for each in dscores]
        leading = [half(each) for each in scaled]
        both = [
            jnp.concatenate([lead, half(each - lead.astype(jnp.float32))], axis=0)
            for lead, each in zip(leading, scaled)
        ]
        dk = [nn(each, query) for each, query in zip(both, q_wide)]
        dq = [collect(tn(each, jnp.concatenate([key, key], axis=0))) for each, key in zip(both, k_all)]
        dk = [each[:count] + each[count:] for each in dk]
        dv = [each[:, :channels] + each[:, channels:] for each in dv]
        return list(zip(queries, keys, att, dq, dk, dv)), sum(dscores[1:], dscores[0])

    if blocks == 1:
        bias_grad = None
        for row in range(0, own, together):
            results, dscores = attend(range(row, min(row + together, own)), 0)
            for queries, keys, att, dq, dk, dv in results:
                att_ref[queries] = att
                dq_ref[queries] = dq
                dk_ref[keys] = dk
                dv_ref[keys] = dv
            bias_grad = dscores if bias_grad is None else bias_grad + dscores
        bias_ref[...] = bias_grad
    else:
        for ref in (att_ref, dq_ref, dk_ref, dv_ref):
            ref[...] = jnp.zeros_like(ref)

        def each(part):
            def each_row(row, bias_grad):
                ((queries, keys, att, dq, dk, dv),), dscores = attend([row], part)
                att_ref[queries] += att
                dq_ref[queries] += dq
                dk_ref[keys] += dk
                dv_ref[keys] += dv
                return bias_grad + dscores

            bias_grad = lax.fori_loop(0, own, each_row, jnp.zeros((count, block), jnp.float32))
            bias_ref[:, pl.ds(pl.multiple_of(part * block, block), block)] = bias_grad

        repeat(blocks, each)

    many = total > block
    if many:
        adapter_ref[...] = jnp.zeros_like(adapter_ref)

    def finish(step):
        rows = pl.ds(pl.multiple_of(step * block, block), block)
        x = x_ref[rows]
        u = u_ref[rows]
        att = att_ref[rows]
        gate = gate_ref[rows]
        gated = half(gate * att)
        dgate = half(dgated_ref[rows] * att * (gate * (1.0 - gate)))
        dproj = [half(ref[rows]) for ref in (dq_ref, dk_ref, dv_ref)]
        dprojs = jnp.concatenate(dproj, axis=1)
        dall_ref[rows, : 3 * channels] = dprojs
        dall_ref[rows, 3 * channels :] = dgate
        low = half(nt(downs, x))
        dlow = half(nt(ups, dprojs))
        grads = [
            nn(dlow, x),
            nn(half(nt(up_ref[3], u)), gated),
            *[nn(low[index * rank : (index + 1) * rank], dproj[index]) for index in range(3)],
            nn(half(nt(down_ref[3], gated)), u),
        ]
        grads = jnp.concatenate(grads, axis=0)
        adapter_ref[...] = adapter_ref[...] + grads if many else grads

    repeat(total // block, finish)

    side = lax.rem(lax.axis_index("sub"), 2) == 0
    split = adapter_ref.shape[0] // 2
    keep_ref[...] = jnp.where(side, adapter_ref[:split], adapter_ref[split:])
    give_ref[...] = jnp.where(side, adapter_ref[split:], adapter_ref[:split])


def cells_kernel(
    dall_ref, bias_ref, weight_ref, down_ref, up_ref, send_ref, rows_ref, cells_ref, bias_rows_ref, *, own
):
    peers = send_ref.shape[0]
    channels = send_ref.shape[2]
    count = own * peers
    cell_rows = own * own
    total = own * count
    bias_rows = bias_ref.shape[1] // lanes
    downs = stacked(down_ref, 3)
    ups = blocked(up_ref, 3)

    def rows_of(step):
        rows = pl.ds(pl.multiple_of(step * block, block), block)
        rows_ref[rows] = (
            nt(dall_ref[rows, : 2 * channels], beside(weight_ref, 0))
            + nt(dall_ref[rows, 2 * channels :], beside(weight_ref, 2))
            + nn(half(nt(dall_ref[rows, : 3 * channels], ups)), downs)
        )

    repeat(total // block, rows_of)
    for row in range(own):
        for place in range(own):
            cells_ref[pl.ds(row * own + place, peers, stride=cell_rows)] = rows_ref[
                pl.ds(place * count + row, peers, stride=own)
            ]
    for part in range(bias_rows):
        bias_rows_ref[pl.ds(part, count, stride=bias_rows)] = bias_ref[:, part * lanes : (part + 1) * lanes]
    send_ref[:, 0:cell_rows] = half(cells_ref[...]).reshape(peers, cell_rows, channels)
    send_ref[:, cell_rows:] = half(bias_rows_ref[...]).reshape(peers, own * bias_rows, lanes)


def pack_kernel(cells_ref, keep_ref, taken_ref, send_ref):
    peers, rows, _ = cells_ref.shape
    send_ref[:, :rows] = cells_ref[...]
    summed = half(keep_ref[...] + taken_ref[...])
    quarter = summed.shape[0] // 2
    for peer in range(peers):
        side = peer % 2
        send_ref[peer, rows:] = summed[side * quarter : (side + 1) * quarter]


def adapter_kernel(recv_ref, out_ref, *, offset):
    quarter = out_ref.shape[0] // 2
    for side in range(2):
        total = recv_ref[side, offset:].astype(jnp.float32)
        for peer in range(side + 2, recv_ref.shape[0], 2):
            total = total + recv_ref[peer, offset:].astype(jnp.float32)
        out_ref[side * quarter : (side + 1) * quarter] = total


def final_kernel(mine_ref, theirs_ref, down_ref, up_ref):
    side = lax.rem(lax.axis_index("sub"), 2) == 0
    quarter = mine_ref.shape[0] // 2
    for index, ref in enumerate((down_ref, up_ref)):
        mine = mine_ref[index * quarter : (index + 1) * quarter]
        theirs = theirs_ref[index * quarter : (index + 1) * quarter]
        ref[:quarter] = jnp.where(side, mine, theirs)
        ref[quarter:] = jnp.where(side, theirs, mine)


def after_kernel(
    recv_ref, unit_ref, inverse_ref, gain_ref, bias_weight_ref, out_ref, rows_ref, cells_ref, bias_ref
):
    own, count, channels = out_ref.shape
    peers = count // own
    heads = bias_weight_ref.shape[0]
    cell_rows = own * own
    bias_rows = heads * count // lanes
    cells_ref[...] = recv_ref[:, :cell_rows].astype(jnp.float32).reshape(own * count, channels)
    for row in range(own):
        for place in range(own):
            rows_ref[pl.ds(row * count + place, peers, stride=own)] = cells_ref[
                pl.ds(row * own + place, peers, stride=cell_rows)
            ]
    summed = recv_ref[0, cell_rows : cell_rows + own * bias_rows].astype(jnp.float32)
    for peer in range(1, peers):
        summed = summed + recv_ref[peer, cell_rows : cell_rows + own * bias_rows].astype(jnp.float32)
    bias_ref[...] = summed
    for row in range(own):
        pieces = []
        for head in range(heads):
            if count < lanes:
                each = lanes // count
                place = (head % each) * count
                line = row * bias_rows + head // each
                pieces.append(bias_ref[line : line + 1, place : place + count])
            else:
                parts = count // lanes
                line = row * bias_rows + head * parts
                pieces.append(
                    jnp.concatenate([bias_ref[line + part : line + part + 1] for part in range(parts)], axis=1)
                )
        bias_grad = half(jnp.concatenate(pieces, axis=0))
        rows = slice(row * count, (row + 1) * count)
        unit = unit_ref[rows]
        grad = (rows_ref[rows] + tn(bias_grad, bias_weight_ref[...])) * gain_ref[...]
        along = jnp.mean(grad * unit, axis=-1, keepdims=True)
        result = inverse_ref[rows] * (grad - jnp.mean(grad, axis=-1, keepdims=True) - unit * along)
        out_ref[row] = half(result)


def swap_cores(values):
    size = lax.axis_size("sub")
    return lax.ppermute(values, "sub", [(place, place ^ 1) for place in range(size)])


def exchange(values):
    return lax.all_to_all(values, group_axes, split_axis=0, concat_axis=0, tiled=True)


def local(
    pair,
    cotangent,
    residue_mask,
    chain_labels,
    gain,
    projection_weight,
    bias_weight,
    output_weight,
    position_bias_table,
    adapter_down_maps,
    adapter_up_maps,
):
    own, count, channels = pair.shape
    peers = count // own
    heads = position_bias_table.shape[0]
    rank = adapter_up_maps.shape[1]
    total = own * count
    cell_rows = own * own
    bias_rows = heads * count // lanes
    adapter_rows = 8 * rank
    adapter_chunk = adapter_rows // 4
    bias_chunk = own * bias_rows
    f32, bf16 = jnp.float32, jnp.bfloat16
    gain_row = gain.reshape(1, channels)
    bias_weight_t = bias_weight.T
    downs = jnp.swapaxes(adapter_down_maps, 1, 2)
    params = pltpu.CompilerParams(vmem_limit_bytes=(16 if total <= 1024 else 56) * 1024 * 1024)

    first_send, unit, inverse, gain_kept, bias_weight_kept = pl.pallas_call(
        before_kernel,
        out_shape=(
            jax.ShapeDtypeStruct((peers, 2 * cell_rows + bias_chunk, channels), bf16),
            jax.ShapeDtypeStruct((total, channels), f32),
            jax.ShapeDtypeStruct((total, 1), f32),
            jax.ShapeDtypeStruct((1, channels), f32),
            jax.ShapeDtypeStruct((heads, channels), bf16),
        ),
        in_specs=[hbm] * 8,
        out_specs=(vmem,) * 5,
        scratch_shapes=[
            pltpu.VMEM((total, channels), f32),
            pltpu.VMEM((total, channels), f32),
            pltpu.VMEM((bias_chunk, lanes), f32),
            pltpu.SMEM((count,), jnp.int32),
            pltpu.SMEM((count,), jnp.int32),
            pltpu.VMEM((1, count), jnp.int32),
            pltpu.VMEM(pair.shape, bf16),
            pltpu.VMEM(pair.shape, bf16),
            pltpu.VMEM(position_bias_table.shape, f32),
            pltpu.SemaphoreType.DMA((8,)),
        ],
        compiler_params=params,
        name="before",
    )(
        *(
            pltpu.with_memory_space_constraint(value, pltpu.HBM)
            for value in (
                residue_mask, chain_labels, chain_labels.reshape(1, count), pair, cotangent, gain_row,
                bias_weight_t, position_bias_table,
            )
        )
    )
    first_recv = exchange(first_send)
    dall, bias_grad, keep, give = pl.pallas_call(
        functools.partial(middle_kernel, own=own, heads=heads),
        out_shape=(
            jax.ShapeDtypeStruct((total, 4 * channels), bf16),
            jax.ShapeDtypeStruct((count, heads * count), f32),
            jax.ShapeDtypeStruct((adapter_rows // 2, channels), f32),
            jax.ShapeDtypeStruct((adapter_rows // 2, channels), f32),
        ),
        in_specs=[vmem] * 5,
        out_specs=(vmem,) * 4,
        scratch_shapes=[
            pltpu.VMEM((total, channels), f32),
            *[pltpu.VMEM((total, channels), bf16)] * 7,
            *[pltpu.VMEM((total, channels), f32)] * 6,
            pltpu.VMEM((count * bias_rows, lanes), f32),
            pltpu.VMEM((adapter_rows, channels), f32),
        ],
        compiler_params=params,
        name="middle",
    )(first_recv, projection_weight, output_weight, downs, adapter_up_maps)
    taken = swap_cores(give)
    cells = pl.pallas_call(
        functools.partial(cells_kernel, own=own),
        out_shape=jax.ShapeDtypeStruct((peers, cell_rows + bias_chunk, channels), bf16),
        in_specs=[vmem] * 5,
        out_specs=vmem,
        scratch_shapes=[
            pltpu.VMEM((total, channels), f32),
            pltpu.VMEM((total, channels), f32),
            pltpu.VMEM((count * bias_rows, lanes), f32),
        ],
        compiler_params=params,
        cost_estimate=pl.CostEstimate(
            flops=10 * total * channels * channels, bytes_accessed=40 * total * channels, transcendentals=0
        ),
        name="cells",
    )(dall, bias_grad, projection_weight, downs, adapter_up_maps)
    second_send = pl.pallas_call(
        pack_kernel,
        out_shape=jax.ShapeDtypeStruct((peers, cell_rows + bias_chunk + adapter_chunk, channels), bf16),
        in_specs=[vmem] * 3,
        out_specs=vmem,
        compiler_params=params,
        name="pack",
    )(cells, keep, taken)
    second_recv = exchange(second_send)
    mine = pl.pallas_call(
        functools.partial(adapter_kernel, offset=cell_rows + bias_chunk),
        out_shape=jax.ShapeDtypeStruct((adapter_rows // 2, channels), f32),
        in_specs=[vmem],
        out_specs=vmem,
        compiler_params=params,
        name="adapters",
    )(second_recv)
    theirs = swap_cores(mine)
    pair_grad = pl.pallas_call(
        after_kernel,
        out_shape=jax.ShapeDtypeStruct((own, count, channels), bf16),
        in_specs=[vmem] * 5,
        out_specs=vmem,
        scratch_shapes=[
            pltpu.VMEM((total, channels), f32),
            pltpu.VMEM((total, channels), f32),
            pltpu.VMEM((bias_chunk, lanes), f32),
        ],
        compiler_params=params,
        cost_estimate=pl.CostEstimate(
            flops=20 * total * channels, bytes_accessed=20 * total * channels, transcendentals=0
        ),
        name="after",
    )(second_recv, unit, inverse, gain_kept, bias_weight_kept)
    down_grad, up_grad = pl.pallas_call(
        final_kernel,
        out_shape=(jax.ShapeDtypeStruct((adapter_rows // 2, channels), f32),) * 2,
        in_specs=[vmem] * 2,
        out_specs=(vmem,) * 2,
        compiler_params=params,
        name="final",
    )(mine, theirs)
    return (
        pair_grad,
        jnp.swapaxes(down_grad.reshape(4, rank, channels), 1, 2),
        up_grad.reshape(4, rank, channels),
    )


def solution(mesh):
    return jax.shard_map(
        local,
        mesh=mesh,
        in_specs=(
            P(("groups", "dap", "sub"), None, None),
            P(("groups", "dap", "sub"), None, None),
            P("groups"),
            P("groups"),
            P(),
            P(),
            P(),
            P(),
            P(),
            P(),
            P(),
        ),
        out_specs=(
            P(("groups", "dap", "sub"), None, None),
            P("groups", None, None),
            P("groups", None, None),
        ),
        check_vma=False,
    )
```

```python
import functools
import math

import jax
import jax.numpy as jnp
from jax import lax
from jax.experimental import pallas as pl
from jax.experimental.pallas import tpu as pltpu
from jax.sharding import PartitionSpec as P

epsilon = 1e-05
lanes = 128
block = 256
masked_bias = -3e38
together = 4
group_axes = ("dap", "sub")
vmem = pl.BlockSpec(memory_space=pltpu.VMEM)
hbm = pl.BlockSpec(memory_space=pltpu.HBM)


def nn(left, right):
    return jnp.dot(left, right, preferred_element_type=jnp.float32)


def nt(left, right):
    return lax.dot_general(left, right, (((1,), (1,)), ((), ())), preferred_element_type=jnp.float32)


def tn(left, right):
    return lax.dot_general(left, right, (((0,), (0,)), ((), ())), preferred_element_type=jnp.float32)


def half(values):
    return values.astype(jnp.bfloat16)


def repeat(count, body):
    if count == 1:
        body(0)
    else:
        lax.fori_loop(0, count, lambda step, carry: (body(step), carry)[1], 0)


def before_kernel(
    mask_hbm, label_hbm, label_row_hbm, pair_hbm, cot_hbm, gain_hbm, bias_weight_hbm, table_hbm,
    send_ref, unit_ref, inverse_ref, gain_ref, bias_weight_ref,
    normed_ref, cells_ref, bias_ref, mask_ref, label_ref, label_row_ref, pair_ref, cot_ref, table_ref, sems,
):
    copies = [
        pltpu.make_async_copy(source, target, sems.at[index])
        for index, (source, target) in enumerate((
            (pair_hbm, pair_ref), (mask_hbm, mask_ref), (label_hbm, label_ref), (label_row_hbm, label_row_ref),
            (gain_hbm, gain_ref), (bias_weight_hbm, bias_weight_ref), (table_hbm, table_ref), (cot_hbm, cot_ref),
        ))
    ]
    for copy in copies:
        copy.start()
    for copy in copies[1:-1]:
        copy.wait()
    own, count, channels = pair_ref.shape
    peers = count // own
    heads, bins = table_ref.shape
    reach = (bins - 2) // 2
    first = lax.axis_index(group_axes) * own
    bias_rows = heads * count // lanes
    gain = gain_ref[...]
    key_pos = lax.broadcasted_iota(jnp.int32, (1, count), 1)
    bin_ids = lax.broadcasted_iota(jnp.int32, (bins, count), 0)
    table = table_ref[...]
    table_parts = []
    for _ in range(3):
        table_parts.append(half(table))
        table = table - table_parts[-1].astype(jnp.float32)
    table_parts = jnp.concatenate(table_parts, axis=0)

    def relative_bias(here):
        same = label_row_ref[...] == label_ref[here]
        offset = jnp.clip(here - key_pos, -reach, reach) + reach
        onehot = half((bin_ids == jnp.where(same, offset, bins - 1)).astype(jnp.float32))
        found = nn(table_parts, onehot)
        return found[:heads] + found[heads : 2 * heads] + found[2 * heads :]

    relative = [relative_bias(first + row) for row in range(own)]
    copies[0].wait()
    for row in range(own):
        here = first + row
        values = pair_ref[row].astype(jnp.float32)
        centred = values - jnp.mean(values, axis=-1, keepdims=True)
        inverse = lax.rsqrt(jnp.mean(centred * centred, axis=-1, keepdims=True) + epsilon)
        unit = centred * inverse
        normed = unit * gain
        unit_ref[row * count : (row + 1) * count] = unit
        inverse_ref[row * count : (row + 1) * count] = inverse
        normed_ref[row * count : (row + 1) * count] = normed
        bias = half(nt(bias_weight_ref[...], half(normed)) + relative[row]).astype(jnp.float32)
        bias = jnp.where(mask_ref[here] > 0, bias, masked_bias)
        for head in range(heads):
            if count < lanes:
                each = lanes // count
                place = (head % each) * count
                bias_ref[row * bias_rows + head // each, place : place + count] = bias[head]
            else:
                for part in range(count // lanes):
                    bias_ref[row * bias_rows + head * (count // lanes) + part, :] = bias[
                        head, part * lanes : (part + 1) * lanes
                    ]
    cell_rows = own * own

    def scatter():
        for row in range(own):
            for place in range(own):
                cells_ref[pl.ds(row * own + place, peers, stride=cell_rows)] = normed_ref[
                    pl.ds(row * count + place, peers, stride=own)
                ]
        return half(cells_ref[...]).reshape(peers, cell_rows, channels)

    send_ref[:, 0:cell_rows] = scatter()
    copies[-1].wait()
    for row in range(own):
        normed_ref[row * count : (row + 1) * count] = cot_ref[row].astype(jnp.float32)
    send_ref[:, cell_rows : 2 * cell_rows] = scatter()
    bias_all = half(bias_ref[...])
    send_ref[:, 2 * cell_rows :] = jnp.broadcast_to(bias_all[None], (peers, *bias_all.shape))


def stacked(maps_ref, count):
    return jnp.concatenate([maps_ref[index] for index in range(count)], axis=0)


def blocked(maps_ref, count):
    empty = jnp.zeros_like(maps_ref[0])
    return jnp.concatenate(
        [
            jnp.concatenate([maps_ref[index] if place == index else empty for place in range(count)], axis=1)
            for index in range(count)
        ],
        axis=0,
    )


def beside(weight_ref, first):
    return jnp.concatenate([weight_ref[first], weight_ref[first + 1]], axis=1)


def adapter_half(given, target_ref, x_ref, u_ref, gate_ref, att_ref, dprojs_ref, down_ref, up_ref):
    total, channels = x_ref.shape
    rank = down_ref.shape[1]
    steps = total // block
    first = lax.rem(lax.axis_index("sub"), 2) == 0
    if steps > 1:
        target_ref[...] = jnp.zeros_like(target_ref)

    def upper(x, u, gated, dprojs):
        low = half(nt(stacked(down_ref, 3), x))
        return [
            *[
                nn(low[index * rank : (index + 1) * rank], dprojs[:, index * channels : (index + 1) * channels])
                for index in range(3)
            ],
            nn(half(nt(down_ref[3], gated)), u),
        ]

    def lower(x, u, gated, dprojs):
        return [nn(half(nt(blocked(up_ref, 3), dprojs)), x), nn(half(nt(up_ref[3], u)), gated)]

    def step_of(part):
        def step(index):
            rows = pl.ds(pl.multiple_of(index * block, block), block)
            gated = half(gate_ref[rows] * att_ref[rows])
            found = jnp.concatenate(part(x_ref[rows], u_ref[rows], gated, dprojs_ref[rows]), axis=0)
            target_ref[...] = target_ref[...] + found if steps > 1 else found

        return step

    @pl.when(first == given)
    def _():
        repeat(steps, step_of(upper))

    @pl.when(first != given)
    def _():
        repeat(steps, step_of(lower))


def middle_kernel(
    recv_ref, weight_ref, out_weight_ref, down_ref, up_ref,
    dprojs_ref, x_ref, u_ref, gate_ref, dgated_ref, att_ref, bias_ref, give_ref,
    rows_ref, q_ref, k_ref, v_ref, da_ref, da2_ref, dq_ref, dk_ref, dv_ref, gathered_ref,
    *, own, heads,
):
    peers = recv_ref.shape[0]
    channels = recv_ref.shape[2]
    count = own * peers
    cell_rows = own * own
    width = channels // heads
    scale = 1.0 / math.sqrt(width)
    bias_rows = heads * count // lanes
    total = own * count
    joint = min(count, block)
    joint_heads = block // joint

    for target, offset in ((x_ref, 0), (u_ref, cell_rows)):
        rows_ref[...] = recv_ref[:, offset : offset + cell_rows].astype(jnp.float32).reshape(total, channels)
        for place in range(own):
            target[place * count : (place + 1) * count] = half(rows_ref[pl.ds(place, count, stride=own)])
    gathered = recv_ref[:, 2 * cell_rows :].astype(jnp.float32)
    gathered_ref[...] = gathered.reshape(count * bias_rows, lanes)
    for part in range(bias_rows):
        bias_ref[:, part * lanes : (part + 1) * lanes] = gathered_ref[pl.ds(part, count, stride=bias_rows)]

    downs = stacked(down_ref, 3)
    ups = blocked(up_ref, 3)

    def project(step):
        rows = pl.ds(pl.multiple_of(step * block, block), block)
        x = x_ref[rows]
        u = u_ref[rows]
        update = nn(half(nt(x, downs)), ups)
        pair01 = nn(x, beside(weight_ref, 0))
        pair23 = nn(x, beside(weight_ref, 2))
        q_ref[rows] = half(pair01[:, :channels] + update[:, :channels])
        k_ref[rows] = half(pair01[:, channels:] + update[:, channels : 2 * channels])
        v_ref[rows] = half(pair23[:, :channels] + update[:, 2 * channels :])
        gate = jax.nn.sigmoid(pair23[:, channels:])
        dgated = nt(u, out_weight_ref[...]) + nn(half(nt(u, up_ref[3])), down_ref[3])
        gate_ref[rows] = gate
        dgated_ref[rows] = dgated
        dattended = dgated * gate
        leading = half(dattended)
        da_ref[rows] = leading
        da2_ref[rows] = half(dattended - leading.astype(jnp.float32))

    repeat(total // block, project)

    head_of = lax.broadcasted_iota(jnp.int32, (1, channels), 1) // width
    blocks = heads * count // block

    def attend(rows, part):
        start = part * block // count
        column = pl.multiple_of(part * block, block)
        first = 0 if count <= block else pl.multiple_of(lax.rem(part * block, count), block)
        queries = [pl.ds(row * count + first, joint) for row in rows]
        keys = [pl.ds(row * count, count) for row in rows]
        spots = [(head_of == start + head).astype(jnp.float32) for head in range(joint_heads)]
        marks = [half(spot) for spot in spots]

        def spread(values):
            return jnp.concatenate([values * mark for mark in marks], axis=0)

        def collect(values):
            return sum(values[head * joint : (head + 1) * joint] * spots[head] for head in range(joint_heads))

        bias = bias_ref[:, pl.ds(column, block)]
        valid = bias > -1e38
        q_wide = [spread(q_ref[at]) for at in queries]
        da_wide = [jnp.concatenate([spread(da_ref[at]), spread(da2_ref[at])], axis=1) for at in queries]
        k_all = [k_ref[at] for at in keys]
        v_all = [v_ref[at] for at in keys]
        scores = [
            jnp.where(valid, nt(key, query) * scale + bias, -1000000000.0) for key, query in zip(k_all, q_wide)
        ]
        dchances = [
            half(nt(jnp.concatenate([value, value], axis=1), da)).astype(jnp.float32)
            for value, da in zip(v_all, da_wide)
        ]
        powers = [jnp.exp(each - jnp.max(each, axis=0, keepdims=True)) for each in scores]
        chances = [each * (1.0 / jnp.sum(each, axis=0, keepdims=True)) for each in powers]
        rounded = [half(each) for each in chances]
        att = [collect(tn(each, value)) for each, value in zip(rounded, v_all)]
        dv = [nn(each, da) for each, da in zip(rounded, da_wide)]
        inner = [left * right for left, right in zip(dchances, chances)]
        dscores = [
            jnp.where(valid, left - right * jnp.sum(left, axis=0, keepdims=True), 0.0)
            for left, right in zip(inner, chances)
        ]
        scaled = [each * scale for each in dscores]
        leading = [half(each) for each in scaled]
        both = [
            jnp.concatenate([lead, half(each - lead.astype(jnp.float32))], axis=0)
            for lead, each in zip(leading, scaled)
        ]
        dk = [nn(each, query) for each, query in zip(both, q_wide)]
        dq = [collect(tn(each, jnp.concatenate([key, key], axis=0))) for each, key in zip(both, k_all)]
        dk = [each[:count] + each[count:] for each in dk]
        dv = [each[:, :channels] + each[:, channels:] for each in dv]
        return list(zip(queries, keys, att, dq, dk, dv)), sum(dscores[1:], dscores[0])

    if blocks == 1:
        bias_grad = None
        for row in range(0, own, together):
            results, dscores = attend(range(row, min(row + together, own)), 0)
            for queries, keys, att, dq, dk, dv in results:
                att_ref[queries] = att
                dq_ref[queries] = dq
                dk_ref[keys] = dk
                dv_ref[keys] = dv
            bias_grad = dscores if bias_grad is None else bias_grad + dscores
        bias_ref[...] = bias_grad
    else:
        for ref in (att_ref, dq_ref, dk_ref, dv_ref):
            ref[...] = jnp.zeros_like(ref)

        def each(part):
            def each_row(row, bias_grad):
                ((queries, keys, att, dq, dk, dv),), dscores = attend([row], part)
                att_ref[queries] += att
                dq_ref[queries] += dq
                dk_ref[keys] += dk
                dv_ref[keys] += dv
                return bias_grad + dscores

            bias_grad = lax.fori_loop(0, own, each_row, jnp.zeros((count, block), jnp.float32))
            bias_ref[:, pl.ds(pl.multiple_of(part * block, block), block)] = bias_grad

        repeat(blocks, each)

    def finish(step):
        rows = pl.ds(pl.multiple_of(step * block, block), block)
        for index, ref in enumerate((dq_ref, dk_ref, dv_ref)):
            dprojs_ref[rows, index * channels : (index + 1) * channels] = half(ref[rows])

    repeat(total // block, finish)
    adapter_half(True, give_ref, x_ref, u_ref, gate_ref, att_ref, dprojs_ref, down_ref, up_ref)


def cells_kernel(
    dprojs_ref, x_ref, u_ref, gate_ref, dgated_ref, att_ref, bias_ref, weight_ref, down_ref, up_ref,
    send_ref, keep_ref, rows_ref, cells_ref, bias_rows_ref, *, own
):
    peers = send_ref.shape[0]
    channels = send_ref.shape[2]
    count = own * peers
    cell_rows = own * own
    total = own * count
    bias_rows = bias_ref.shape[1] // lanes
    downs = stacked(down_ref, 3)
    ups = blocked(up_ref, 3)

    def rows_of(step):
        rows = pl.ds(pl.multiple_of(step * block, block), block)
        gate = gate_ref[rows]
        dgate = half(dgated_ref[rows] * att_ref[rows] * (gate * (1.0 - gate)))
        dprojs = dprojs_ref[rows]
        rows_ref[rows] = (
            nt(dprojs[:, : 2 * channels], beside(weight_ref, 0))
            + nt(jnp.concatenate([dprojs[:, 2 * channels :], dgate], axis=1), beside(weight_ref, 2))
            + nn(half(nt(dprojs, ups)), downs)
        )

    repeat(total // block, rows_of)
    adapter_half(False, keep_ref, x_ref, u_ref, gate_ref, att_ref, dprojs_ref, down_ref, up_ref)
    for row in range(own):
        for place in range(own):
            cells_ref[pl.ds(row * own + place, peers, stride=cell_rows)] = rows_ref[
                pl.ds(place * count + row, peers, stride=own)
            ]
    for part in range(bias_rows):
        bias_rows_ref[pl.ds(part, count, stride=bias_rows)] = bias_ref[:, part * lanes : (part + 1) * lanes]
    send_ref[:, 0:cell_rows] = half(cells_ref[...]).reshape(peers, cell_rows, channels)
    send_ref[:, cell_rows:] = half(bias_rows_ref[...]).reshape(peers, own * bias_rows, lanes)


def pack_kernel(cells_ref, keep_ref, taken_ref, send_ref):
    peers, rows, _ = cells_ref.shape
    send_ref[:, :rows] = cells_ref[...]
    summed = half(keep_ref[...] + taken_ref[...])
    quarter = summed.shape[0] // 2
    for peer in range(peers):
        side = peer % 2
        send_ref[peer, rows:] = summed[side * quarter : (side + 1) * quarter]


def adapter_kernel(recv_ref, out_ref, *, offset):
    quarter = out_ref.shape[0] // 2
    for side in range(2):
        total = recv_ref[side, offset:].astype(jnp.float32)
        for peer in range(side + 2, recv_ref.shape[0], 2):
            total = total + recv_ref[peer, offset:].astype(jnp.float32)
        out_ref[side * quarter : (side + 1) * quarter] = total


def final_kernel(mine_ref, theirs_ref, down_ref, up_ref):
    side = lax.rem(lax.axis_index("sub"), 2) == 0
    quarter = mine_ref.shape[0] // 2
    for index, ref in enumerate((down_ref, up_ref)):
        mine = mine_ref[index * quarter : (index + 1) * quarter]
        theirs = theirs_ref[index * quarter : (index + 1) * quarter]
        ref[:quarter] = jnp.where(side, mine, theirs)
        ref[quarter:] = jnp.where(side, theirs, mine)


def after_kernel(
    recv_ref, unit_ref, inverse_ref, gain_ref, bias_weight_ref, out_ref, rows_ref, cells_ref, bias_ref
):
    own, count, channels = out_ref.shape
    peers = count // own
    heads = bias_weight_ref.shape[0]
    cell_rows = own * own
    bias_rows = heads * count // lanes
    cells_ref[...] = recv_ref[:, :cell_rows].astype(jnp.float32).reshape(own * count, channels)
    for row in range(own):
        for place in range(own):
            rows_ref[pl.ds(row * count + place, peers, stride=own)] = cells_ref[
                pl.ds(row * own + place, peers, stride=cell_rows)
            ]
    summed = recv_ref[0, cell_rows : cell_rows + own * bias_rows].astype(jnp.float32)
    for peer in range(1, peers):
        summed = summed + recv_ref[peer, cell_rows : cell_rows + own * bias_rows].astype(jnp.float32)
    bias_ref[...] = summed
    for row in range(own):
        pieces = []
        for head in range(heads):
            if count < lanes:
                each = lanes // count
                place = (head % each) * count
                line = row * bias_rows + head // each
                pieces.append(bias_ref[line : line + 1, place : place + count])
            else:
                parts = count // lanes
                line = row * bias_rows + head * parts
                pieces.append(
                    jnp.concatenate([bias_ref[line + part : line + part + 1] for part in range(parts)], axis=1)
                )
        bias_grad = half(jnp.concatenate(pieces, axis=0))
        rows = slice(row * count, (row + 1) * count)
        unit = unit_ref[rows]
        grad = (rows_ref[rows] + tn(bias_grad, bias_weight_ref[...])) * gain_ref[...]
        along = jnp.mean(grad * unit, axis=-1, keepdims=True)
        result = inverse_ref[rows] * (grad - jnp.mean(grad, axis=-1, keepdims=True) - unit * along)
        out_ref[row] = half(result)


def swap_cores(values):
    size = lax.axis_size("sub")
    return lax.ppermute(values, "sub", [(place, place ^ 1) for place in range(size)])


def exchange(values):
    return lax.all_to_all(values, group_axes, split_axis=0, concat_axis=0, tiled=True)


def local(
    pair,
    cotangent,
    residue_mask,
    chain_labels,
    gain,
    projection_weight,
    bias_weight,
    output_weight,
    position_bias_table,
    adapter_down_maps,
    adapter_up_maps,
):
    own, count, channels = pair.shape
    peers = count // own
    heads = position_bias_table.shape[0]
    rank = adapter_up_maps.shape[1]
    total = own * count
    cell_rows = own * own
    bias_rows = heads * count // lanes
    adapter_rows = 8 * rank
    adapter_chunk = adapter_rows // 4
    bias_chunk = own * bias_rows
    f32, bf16 = jnp.float32, jnp.bfloat16
    gain_row = gain.reshape(1, channels)
    bias_weight_t = bias_weight.T
    downs = jnp.swapaxes(adapter_down_maps, 1, 2)
    params = pltpu.CompilerParams(vmem_limit_bytes=(16 if total <= 1024 else 56) * 1024 * 1024)

    first_send, unit, inverse, gain_kept, bias_weight_kept = pl.pallas_call(
        before_kernel,
        out_shape=(
            jax.ShapeDtypeStruct((peers, 2 * cell_rows + bias_chunk, channels), bf16),
            jax.ShapeDtypeStruct((total, channels), f32),
            jax.ShapeDtypeStruct((total, 1), f32),
            jax.ShapeDtypeStruct((1, channels), f32),
            jax.ShapeDtypeStruct((heads, channels), bf16),
        ),
        in_specs=[hbm] * 8,
        out_specs=(vmem,) * 5,
        scratch_shapes=[
            pltpu.VMEM((total, channels), f32),
            pltpu.VMEM((total, channels), f32),
            pltpu.VMEM((bias_chunk, lanes), f32),
            pltpu.SMEM((count,), jnp.int32),
            pltpu.SMEM((count,), jnp.int32),
            pltpu.VMEM((1, count), jnp.int32),
            pltpu.VMEM(pair.shape, bf16),
            pltpu.VMEM(pair.shape, bf16),
            pltpu.VMEM(position_bias_table.shape, f32),
            pltpu.SemaphoreType.DMA((8,)),
        ],
        compiler_params=params,
        name="before",
    )(
        *(
            pltpu.with_memory_space_constraint(value, pltpu.HBM)
            for value in (
                residue_mask, chain_labels, chain_labels.reshape(1, count), pair, cotangent, gain_row,
                bias_weight_t, position_bias_table,
            )
        )
    )
    first_recv = exchange(first_send)
    *kept, give = pl.pallas_call(
        functools.partial(middle_kernel, own=own, heads=heads),
        out_shape=(
            jax.ShapeDtypeStruct((total, 3 * channels), bf16),
            *[jax.ShapeDtypeStruct((total, channels), bf16)] * 2,
            *[jax.ShapeDtypeStruct((total, channels), f32)] * 3,
            jax.ShapeDtypeStruct((count, heads * count), f32),
            jax.ShapeDtypeStruct((adapter_rows // 2, channels), f32),
        ),
        in_specs=[vmem] * 5,
        out_specs=(vmem,) * 8,
        scratch_shapes=[
            pltpu.VMEM((total, channels), f32),
            *[pltpu.VMEM((total, channels), bf16)] * 5,
            *[pltpu.VMEM((total, channels), f32)] * 3,
            pltpu.VMEM((count * bias_rows, lanes), f32),
        ],
        compiler_params=params,
        name="middle",
    )(first_recv, projection_weight, output_weight, downs, adapter_up_maps)
    taken = swap_cores(give)
    cells, keep = pl.pallas_call(
        functools.partial(cells_kernel, own=own),
        out_shape=(
            jax.ShapeDtypeStruct((peers, cell_rows + bias_chunk, channels), bf16),
            jax.ShapeDtypeStruct((adapter_rows // 2, channels), f32),
        ),
        in_specs=[vmem] * 10,
        out_specs=(vmem,) * 2,
        scratch_shapes=[
            pltpu.VMEM((total, channels), f32),
            pltpu.VMEM((total, channels), f32),
            pltpu.VMEM((count * bias_rows, lanes), f32),
        ],
        compiler_params=params,
        cost_estimate=pl.CostEstimate(
            flops=10 * total * channels * channels, bytes_accessed=40 * total * channels, transcendentals=0
        ),
        name="cells",
    )(*kept, projection_weight, downs, adapter_up_maps)
    second_send = pl.pallas_call(
        pack_kernel,
        out_shape=jax.ShapeDtypeStruct((peers, cell_rows + bias_chunk + adapter_chunk, channels), bf16),
        in_specs=[vmem] * 3,
        out_specs=vmem,
        compiler_params=params,
        name="pack",
    )(cells, keep, taken)
    second_recv = exchange(second_send)
    mine = pl.pallas_call(
        functools.partial(adapter_kernel, offset=cell_rows + bias_chunk),
        out_shape=jax.ShapeDtypeStruct((adapter_rows // 2, channels), f32),
        in_specs=[vmem],
        out_specs=vmem,
        compiler_params=params,
        name="adapters",
    )(second_recv)
    theirs = swap_cores(mine)
    pair_grad = pl.pallas_call(
        after_kernel,
        out_shape=jax.ShapeDtypeStruct((own, count, channels), bf16),
        in_specs=[vmem] * 5,
        out_specs=vmem,
        scratch_shapes=[
            pltpu.VMEM((total, channels), f32),
            pltpu.VMEM((total, channels), f32),
            pltpu.VMEM((bias_chunk, lanes), f32),
        ],
        compiler_params=params,
        cost_estimate=pl.CostEstimate(
            flops=20 * total * channels, bytes_accessed=20 * total * channels, transcendentals=0
        ),
        name="after",
    )(second_recv, unit, inverse, gain_kept, bias_weight_kept)
    down_grad, up_grad = pl.pallas_call(
        final_kernel,
        out_shape=(jax.ShapeDtypeStruct((adapter_rows // 2, channels), f32),) * 2,
        in_specs=[vmem] * 2,
        out_specs=(vmem,) * 2,
        compiler_params=params,
        name="final",
    )(mine, theirs)
    return (
        pair_grad,
        jnp.swapaxes(down_grad.reshape(4, rank, channels), 1, 2),
        up_grad.reshape(4, rank, channels),
    )


def solution(mesh):
    return jax.shard_map(
        local,
        mesh=mesh,
        in_specs=(
            P(("groups", "dap", "sub"), None, None),
            P(("groups", "dap", "sub"), None, None),
            P("groups"),
            P("groups"),
            P(),
            P(),
            P(),
            P(),
            P(),
            P(),
            P(),
        ),
        out_specs=(
            P(("groups", "dap", "sub"), None, None),
            P("groups", None, None),
            P("groups", None, None),
        ),
        check_vma=False,
    )
```

```python
import functools
import math

import jax
import jax.numpy as jnp
from jax import lax
from jax.experimental import pallas as pl
from jax.experimental.pallas import tpu as pltpu
from jax.sharding import PartitionSpec as P

epsilon = 1e-05
lanes = 128
block = 256
masked_bias = -3e38
together = 4
group_axes = ("dap", "sub")
vmem = pl.BlockSpec(memory_space=pltpu.VMEM)
hbm = pl.BlockSpec(memory_space=pltpu.HBM)


def nn(left, right):
    return jnp.dot(left, right, preferred_element_type=jnp.float32)


def nt(left, right):
    return lax.dot_general(left, right, (((1,), (1,)), ((), ())), preferred_element_type=jnp.float32)


def tn(left, right):
    return lax.dot_general(left, right, (((0,), (0,)), ((), ())), preferred_element_type=jnp.float32)


def half(values):
    return values.astype(jnp.bfloat16)


def repeat(count, body):
    if count == 1:
        body(0)
    else:
        lax.fori_loop(0, count, lambda step, carry: (body(step), carry)[1], 0)


def before_kernel(
    mask_hbm, label_hbm, label_row_hbm, pair_hbm, cot_hbm, gain_hbm, bias_weight_hbm, table_hbm,
    send_ref, unit_ref, inverse_ref, gain_ref, bias_weight_ref,
    normed_ref, cells_ref, bias_ref, mask_ref, label_ref, label_row_ref, pair_ref, cot_ref, table_ref, sems,
):
    copies = [
        pltpu.make_async_copy(source, target, sems.at[index])
        for index, (source, target) in enumerate((
            (pair_hbm, pair_ref), (mask_hbm, mask_ref), (label_hbm, label_ref), (label_row_hbm, label_row_ref),
            (gain_hbm, gain_ref), (bias_weight_hbm, bias_weight_ref), (table_hbm, table_ref), (cot_hbm, cot_ref),
        ))
    ]
    for copy in copies:
        copy.start()
    for copy in copies[1:-1]:
        copy.wait()
    own, count, channels = pair_ref.shape
    peers = count // own
    heads, bins = table_ref.shape
    reach = (bins - 2) // 2
    first = lax.axis_index(group_axes) * own
    bias_rows = heads * count // lanes
    gain = gain_ref[...]
    key_pos = lax.broadcasted_iota(jnp.int32, (1, count), 1)
    bin_ids = lax.broadcasted_iota(jnp.int32, (bins, count), 0)
    table = table_ref[...]
    table_parts = []
    for _ in range(3):
        table_parts.append(half(table))
        table = table - table_parts[-1].astype(jnp.float32)
    table_parts = jnp.concatenate(table_parts, axis=0)

    def relative_bias(here):
        same = label_row_ref[...] == label_ref[here]
        offset = jnp.clip(here - key_pos, -reach, reach) + reach
        onehot = half((bin_ids == jnp.where(same, offset, bins - 1)).astype(jnp.float32))
        found = nn(table_parts, onehot)
        return found[:heads] + found[heads : 2 * heads] + found[2 * heads :]

    relative = [relative_bias(first + row) for row in range(own)]
    copies[0].wait()
    for row in range(own):
        here = first + row
        values = pair_ref[row].astype(jnp.float32)
        centred = values - jnp.mean(values, axis=-1, keepdims=True)
        inverse = lax.rsqrt(jnp.mean(centred * centred, axis=-1, keepdims=True) + epsilon)
        unit = centred * inverse
        normed = unit * gain
        unit_ref[row * count : (row + 1) * count] = unit
        inverse_ref[row * count : (row + 1) * count] = inverse
        normed_ref[row * count : (row + 1) * count] = normed
        bias = half(nt(bias_weight_ref[...], half(normed)) + relative[row]).astype(jnp.float32)
        bias = jnp.where(mask_ref[here] > 0, bias, masked_bias)
        for head in range(heads):
            if count < lanes:
                each = lanes // count
                place = (head % each) * count
                bias_ref[row * bias_rows + head // each, place : place + count] = bias[head]
            else:
                for part in range(count // lanes):
                    bias_ref[row * bias_rows + head * (count // lanes) + part, :] = bias[
                        head, part * lanes : (part + 1) * lanes
                    ]
    cell_rows = own * own

    def scatter():
        for row in range(own):
            for place in range(own):
                cells_ref[pl.ds(row * own + place, peers, stride=cell_rows)] = normed_ref[
                    pl.ds(row * count + place, peers, stride=own)
                ]
        return half(cells_ref[...]).reshape(peers, cell_rows, channels)

    send_ref[:, 0:cell_rows] = scatter()
    copies[-1].wait()
    for row in range(own):
        normed_ref[row * count : (row + 1) * count] = cot_ref[row].astype(jnp.float32)
    send_ref[:, cell_rows : 2 * cell_rows] = scatter()
    bias_all = half(bias_ref[...])
    send_ref[:, 2 * cell_rows :] = jnp.broadcast_to(bias_all[None], (peers, *bias_all.shape))


def stacked(maps_ref, count):
    return jnp.concatenate([maps_ref[index] for index in range(count)], axis=0)


def blocked(maps_ref, count):
    empty = jnp.zeros_like(maps_ref[0])
    return jnp.concatenate(
        [
            jnp.concatenate([maps_ref[index] if place == index else empty for place in range(count)], axis=1)
            for index in range(count)
        ],
        axis=0,
    )


def beside(weight_ref, first):
    return jnp.concatenate([weight_ref[first], weight_ref[first + 1]], axis=1)


def adapter_half(given, target_ref, x_ref, u_ref, gate_ref, att_ref, dprojs_ref, down_ref, up_ref):
    total, channels = x_ref.shape
    rank = down_ref.shape[1]
    steps = total // block
    first = lax.rem(lax.axis_index("sub"), 2) == 0
    if steps > 1:
        target_ref[...] = jnp.zeros_like(target_ref)

    def upper(x, u, gated, dprojs):
        low = half(nt(stacked(down_ref, 3), x))
        return [
            *[
                nn(low[index * rank : (index + 1) * rank], dprojs[:, index * channels : (index + 1) * channels])
                for index in range(3)
            ],
            nn(half(nt(down_ref[3], gated)), u),
        ]

    def lower(x, u, gated, dprojs):
        return [nn(half(nt(blocked(up_ref, 3), dprojs)), x), nn(half(nt(up_ref[3], u)), gated)]

    def step_of(part):
        def step(index):
            rows = pl.ds(pl.multiple_of(index * block, block), block)
            gated = half(gate_ref[rows] * att_ref[rows])
            found = jnp.concatenate(part(x_ref[rows], u_ref[rows], gated, dprojs_ref[rows]), axis=0)
            target_ref[...] = target_ref[...] + found if steps > 1 else found

        return step

    @pl.when(first == given)
    def _():
        repeat(steps, step_of(upper))

    @pl.when(first != given)
    def _():
        repeat(steps, step_of(lower))


def middle_kernel(
    recv_ref, weight_ref, out_weight_ref, down_ref, up_ref,
    dprojs_ref, x_ref, u_ref, gate_ref, dgated_ref, att_ref, bias_ref, give_ref,
    rows_ref, q_ref, k_ref, v_ref, da_ref, da2_ref, dq_ref, dk_ref, dv_ref, gathered_ref,
    *, own, heads,
):
    peers = recv_ref.shape[0]
    channels = recv_ref.shape[2]
    count = own * peers
    cell_rows = own * own
    width = channels // heads
    scale = 1.0 / math.sqrt(width)
    bias_rows = heads * count // lanes
    total = own * count
    joint = min(count, block)
    joint_heads = block // joint

    for target, offset in ((x_ref, 0), (u_ref, cell_rows)):
        rows_ref[...] = recv_ref[:, offset : offset + cell_rows].astype(jnp.float32).reshape(total, channels)
        for place in range(own):
            target[place * count : (place + 1) * count] = half(rows_ref[pl.ds(place, count, stride=own)])
    gathered = recv_ref[:, 2 * cell_rows :].astype(jnp.float32)
    gathered_ref[...] = gathered.reshape(count * bias_rows, lanes)
    for part in range(bias_rows):
        bias_ref[:, part * lanes : (part + 1) * lanes] = gathered_ref[pl.ds(part, count, stride=bias_rows)]

    downs = stacked(down_ref, 3)
    ups = blocked(up_ref, 3)

    spare = jnp.concatenate([ups[:, 2 * channels :], jnp.zeros_like(ups[:, :channels])], axis=1)

    def project(step):
        rows = pl.ds(pl.multiple_of(step * block, block), block)
        x = x_ref[rows]
        u = u_ref[rows]
        joined = jnp.concatenate([x, half(nt(x, downs))], axis=1)
        pair01 = nn(joined, jnp.concatenate([beside(weight_ref, 0), ups[:, : 2 * channels]], axis=0))
        pair23 = nn(joined, jnp.concatenate([beside(weight_ref, 2), spare], axis=0))
        q_ref[rows] = half(pair01[:, :channels])
        k_ref[rows] = half(pair01[:, channels:])
        v_ref[rows] = half(pair23[:, :channels])
        gate = jax.nn.sigmoid(pair23[:, channels:])
        dgated = nt(u, out_weight_ref[...]) + nn(half(nt(u, up_ref[3])), down_ref[3])
        gate_ref[rows] = gate
        dgated_ref[rows] = dgated
        dattended = dgated * gate
        leading = half(dattended)
        da_ref[rows] = leading
        da2_ref[rows] = half(dattended - leading.astype(jnp.float32))

    repeat(total // block, project)

    head_of = lax.broadcasted_iota(jnp.int32, (1, channels), 1) // width
    blocks = heads * count // block

    def attend(rows, part):
        start = part * block // count
        column = pl.multiple_of(part * block, block)
        first = 0 if count <= block else pl.multiple_of(lax.rem(part * block, count), block)
        queries = [pl.ds(row * count + first, joint) for row in rows]
        keys = [pl.ds(row * count, count) for row in rows]
        spots = [(head_of == start + head).astype(jnp.float32) for head in range(joint_heads)]
        marks = [half(spot) for spot in spots]

        def spread(values):
            return jnp.concatenate([values * mark for mark in marks], axis=0)

        def collect(values):
            return sum(values[head * joint : (head + 1) * joint] * spots[head] for head in range(joint_heads))

        bias = bias_ref[:, pl.ds(column, block)]
        valid = bias > -1e38
        q_wide = [spread(q_ref[at]) for at in queries]
        da_wide = [jnp.concatenate([spread(da_ref[at]), spread(da2_ref[at])], axis=1) for at in queries]
        k_all = [k_ref[at] for at in keys]
        v_all = [v_ref[at] for at in keys]
        scores = [
            jnp.where(valid, nt(key, query) * scale + bias, -1000000000.0) for key, query in zip(k_all, q_wide)
        ]
        dchances = [
            half(nt(jnp.concatenate([value, value], axis=1), da)).astype(jnp.float32)
            for value, da in zip(v_all, da_wide)
        ]
        powers = [jnp.exp(each - jnp.max(each, axis=0, keepdims=True)) for each in scores]
        chances = [each * (1.0 / jnp.sum(each, axis=0, keepdims=True)) for each in powers]
        rounded = [half(each) for each in chances]
        att = [collect(tn(each, value)) for each, value in zip(rounded, v_all)]
        dv = [nn(each, da) for each, da in zip(rounded, da_wide)]
        inner = [left * right for left, right in zip(dchances, chances)]
        dscores = [
            jnp.where(valid, left - right * jnp.sum(left, axis=0, keepdims=True), 0.0)
            for left, right in zip(inner, chances)
        ]
        scaled = [each * scale for each in dscores]
        leading = [half(each) for each in scaled]
        both = [
            jnp.concatenate([lead, half(each - lead.astype(jnp.float32))], axis=0)
            for lead, each in zip(leading, scaled)
        ]
        dk = [nn(each, query) for each, query in zip(both, q_wide)]
        dq = [collect(tn(each, jnp.concatenate([key, key], axis=0))) for each, key in zip(both, k_all)]
        dk = [each[:count] + each[count:] for each in dk]
        dv = [each[:, :channels] + each[:, channels:] for each in dv]
        return list(zip(queries, keys, att, dq, dk, dv)), sum(dscores[1:], dscores[0])

    if blocks == 1:
        bias_grad = None
        for row in range(0, own, together):
            results, dscores = attend(range(row, min(row + together, own)), 0)
            for queries, keys, att, dq, dk, dv in results:
                att_ref[queries] = att
                dq_ref[queries] = dq
                dk_ref[keys] = dk
                dv_ref[keys] = dv
            bias_grad = dscores if bias_grad is None else bias_grad + dscores
        bias_ref[...] = bias_grad
    else:
        for ref in (att_ref, dq_ref, dk_ref, dv_ref):
            ref[...] = jnp.zeros_like(ref)

        def each(part):
            def each_row(row, bias_grad):
                ((queries, keys, att, dq, dk, dv),), dscores = attend([row], part)
                att_ref[queries] += att
                dq_ref[queries] += dq
                dk_ref[keys] += dk
                dv_ref[keys] += dv
                return bias_grad + dscores

            bias_grad = lax.fori_loop(0, own, each_row, jnp.zeros((count, block), jnp.float32))
            bias_ref[:, pl.ds(pl.multiple_of(part * block, block), block)] = bias_grad

        repeat(blocks, each)

    def finish(step):
        rows = pl.ds(pl.multiple_of(step * block, block), block)
        for index, ref in enumerate((dq_ref, dk_ref, dv_ref)):
            dprojs_ref[rows, index * channels : (index + 1) * channels] = half(ref[rows])

    repeat(total // block, finish)
    adapter_half(True, give_ref, x_ref, u_ref, gate_ref, att_ref, dprojs_ref, down_ref, up_ref)


def cells_kernel(
    dprojs_ref, x_ref, u_ref, gate_ref, dgated_ref, att_ref, bias_ref, weight_ref, down_ref, up_ref,
    send_ref, keep_ref, rows_ref, cells_ref, bias_rows_ref, *, own
):
    peers = send_ref.shape[0]
    channels = send_ref.shape[2]
    count = own * peers
    cell_rows = own * own
    total = own * count
    bias_rows = bias_ref.shape[1] // lanes
    downs = stacked(down_ref, 3)
    ups = blocked(up_ref, 3)

    def rows_of(step):
        rows = pl.ds(pl.multiple_of(step * block, block), block)
        gate = gate_ref[rows]
        dgate = half(dgated_ref[rows] * att_ref[rows] * (gate * (1.0 - gate)))
        dprojs = dprojs_ref[rows]
        rows_ref[rows] = (
            nt(dprojs[:, : 2 * channels], beside(weight_ref, 0))
            + nt(jnp.concatenate([dprojs[:, 2 * channels :], dgate], axis=1), beside(weight_ref, 2))
            + nn(half(nt(dprojs, ups)), downs)
        )

    repeat(total // block, rows_of)
    adapter_half(False, keep_ref, x_ref, u_ref, gate_ref, att_ref, dprojs_ref, down_ref, up_ref)
    for row in range(own):
        for place in range(own):
            cells_ref[pl.ds(row * own + place, peers, stride=cell_rows)] = rows_ref[
                pl.ds(place * count + row, peers, stride=own)
            ]
    for part in range(bias_rows):
        bias_rows_ref[pl.ds(part, count, stride=bias_rows)] = bias_ref[:, part * lanes : (part + 1) * lanes]
    send_ref[:, 0:cell_rows] = half(cells_ref[...]).reshape(peers, cell_rows, channels)
    send_ref[:, cell_rows:] = half(bias_rows_ref[...]).reshape(peers, own * bias_rows, lanes)


def pack_kernel(cells_ref, keep_ref, taken_ref, send_ref):
    peers, rows, _ = cells_ref.shape
    send_ref[:, :rows] = cells_ref[...]
    summed = half(keep_ref[...] + taken_ref[...])
    quarter = summed.shape[0] // 2
    for peer in range(peers):
        side = peer % 2
        send_ref[peer, rows:] = summed[side * quarter : (side + 1) * quarter]


def adapter_kernel(recv_ref, out_ref, *, offset):
    quarter = out_ref.shape[0] // 2
    for side in range(2):
        total = recv_ref[side, offset:].astype(jnp.float32)
        for peer in range(side + 2, recv_ref.shape[0], 2):
            total = total + recv_ref[peer, offset:].astype(jnp.float32)
        out_ref[side * quarter : (side + 1) * quarter] = total


def final_kernel(mine_ref, theirs_ref, down_ref, up_ref):
    side = lax.rem(lax.axis_index("sub"), 2) == 0
    quarter = mine_ref.shape[0] // 2
    for index, ref in enumerate((down_ref, up_ref)):
        mine = mine_ref[index * quarter : (index + 1) * quarter]
        theirs = theirs_ref[index * quarter : (index + 1) * quarter]
        ref[:quarter] = jnp.where(side, mine, theirs)
        ref[quarter:] = jnp.where(side, theirs, mine)


def after_kernel(
    recv_ref, unit_ref, inverse_ref, gain_ref, bias_weight_ref, out_ref, rows_ref, cells_ref, bias_ref
):
    own, count, channels = out_ref.shape
    peers = count // own
    heads = bias_weight_ref.shape[0]
    cell_rows = own * own
    bias_rows = heads * count // lanes
    cells_ref[...] = recv_ref[:, :cell_rows].astype(jnp.float32).reshape(own * count, channels)
    for row in range(own):
        for place in range(own):
            rows_ref[pl.ds(row * count + place, peers, stride=own)] = cells_ref[
                pl.ds(row * own + place, peers, stride=cell_rows)
            ]
    summed = recv_ref[0, cell_rows : cell_rows + own * bias_rows].astype(jnp.float32)
    for peer in range(1, peers):
        summed = summed + recv_ref[peer, cell_rows : cell_rows + own * bias_rows].astype(jnp.float32)
    bias_ref[...] = summed
    for row in range(own):
        pieces = []
        for head in range(heads):
            if count < lanes:
                each = lanes // count
                place = (head % each) * count
                line = row * bias_rows + head // each
                pieces.append(bias_ref[line : line + 1, place : place + count])
            else:
                parts = count // lanes
                line = row * bias_rows + head * parts
                pieces.append(
                    jnp.concatenate([bias_ref[line + part : line + part + 1] for part in range(parts)], axis=1)
                )
        bias_grad = half(jnp.concatenate(pieces, axis=0))
        rows = slice(row * count, (row + 1) * count)
        unit = unit_ref[rows]
        grad = (rows_ref[rows] + tn(bias_grad, bias_weight_ref[...])) * gain_ref[...]
        along = jnp.mean(grad * unit, axis=-1, keepdims=True)
        result = inverse_ref[rows] * (grad - jnp.mean(grad, axis=-1, keepdims=True) - unit * along)
        out_ref[row] = half(result)


def swap_cores(values):
    size = lax.axis_size("sub")
    return lax.ppermute(values, "sub", [(place, place ^ 1) for place in range(size)])


def exchange(values):
    return lax.all_to_all(values, group_axes, split_axis=0, concat_axis=0, tiled=True)


def local(
    pair,
    cotangent,
    residue_mask,
    chain_labels,
    gain,
    projection_weight,
    bias_weight,
    output_weight,
    position_bias_table,
    adapter_down_maps,
    adapter_up_maps,
):
    own, count, channels = pair.shape
    peers = count // own
    heads = position_bias_table.shape[0]
    rank = adapter_up_maps.shape[1]
    total = own * count
    cell_rows = own * own
    bias_rows = heads * count // lanes
    adapter_rows = 8 * rank
    adapter_chunk = adapter_rows // 4
    bias_chunk = own * bias_rows
    f32, bf16 = jnp.float32, jnp.bfloat16
    gain_row = gain.reshape(1, channels)
    bias_weight_t = bias_weight.T
    downs = jnp.swapaxes(adapter_down_maps, 1, 2)
    params = pltpu.CompilerParams(vmem_limit_bytes=(16 if total <= 1024 else 56) * 1024 * 1024)

    first_send, unit, inverse, gain_kept, bias_weight_kept = pl.pallas_call(
        before_kernel,
        out_shape=(
            jax.ShapeDtypeStruct((peers, 2 * cell_rows + bias_chunk, channels), bf16),
            jax.ShapeDtypeStruct((total, channels), f32),
            jax.ShapeDtypeStruct((total, 1), f32),
            jax.ShapeDtypeStruct((1, channels), f32),
            jax.ShapeDtypeStruct((heads, channels), bf16),
        ),
        in_specs=[hbm] * 8,
        out_specs=(vmem,) * 5,
        scratch_shapes=[
            pltpu.VMEM((total, channels), f32),
            pltpu.VMEM((total, channels), f32),
            pltpu.VMEM((bias_chunk, lanes), f32),
            pltpu.SMEM((count,), jnp.int32),
            pltpu.SMEM((count,), jnp.int32),
            pltpu.VMEM((1, count), jnp.int32),
            pltpu.VMEM(pair.shape, bf16),
            pltpu.VMEM(pair.shape, bf16),
            pltpu.VMEM(position_bias_table.shape, f32),
            pltpu.SemaphoreType.DMA((8,)),
        ],
        compiler_params=params,
        name="before",
    )(
        *(
            pltpu.with_memory_space_constraint(value, pltpu.HBM)
            for value in (
                residue_mask, chain_labels, chain_labels.reshape(1, count), pair, cotangent, gain_row,
                bias_weight_t, position_bias_table,
            )
        )
    )
    first_recv = exchange(first_send)
    *kept, give = pl.pallas_call(
        functools.partial(middle_kernel, own=own, heads=heads),
        out_shape=(
            jax.ShapeDtypeStruct((total, 3 * channels), bf16),
            *[jax.ShapeDtypeStruct((total, channels), bf16)] * 2,
            *[jax.ShapeDtypeStruct((total, channels), f32)] * 3,
            jax.ShapeDtypeStruct((count, heads * count), f32),
            jax.ShapeDtypeStruct((adapter_rows // 2, channels), f32),
        ),
        in_specs=[vmem] * 5,
        out_specs=(vmem,) * 8,
        scratch_shapes=[
            pltpu.VMEM((total, channels), f32),
            *[pltpu.VMEM((total, channels), bf16)] * 5,
            *[pltpu.VMEM((total, channels), f32)] * 3,
            pltpu.VMEM((count * bias_rows, lanes), f32),
        ],
        compiler_params=params,
        name="middle",
    )(first_recv, projection_weight, output_weight, downs, adapter_up_maps)
    taken = swap_cores(give)
    cells, keep = pl.pallas_call(
        functools.partial(cells_kernel, own=own),
        out_shape=(
            jax.ShapeDtypeStruct((peers, cell_rows + bias_chunk, channels), bf16),
            jax.ShapeDtypeStruct((adapter_rows // 2, channels), f32),
        ),
        in_specs=[vmem] * 10,
        out_specs=(vmem,) * 2,
        scratch_shapes=[
            pltpu.VMEM((total, channels), f32),
            pltpu.VMEM((total, channels), f32),
            pltpu.VMEM((count * bias_rows, lanes), f32),
        ],
        compiler_params=params,
        cost_estimate=pl.CostEstimate(
            flops=10 * total * channels * channels, bytes_accessed=40 * total * channels, transcendentals=0
        ),
        name="cells",
    )(*kept, projection_weight, downs, adapter_up_maps)
    second_send = pl.pallas_call(
        pack_kernel,
        out_shape=jax.ShapeDtypeStruct((peers, cell_rows + bias_chunk + adapter_chunk, channels), bf16),
        in_specs=[vmem] * 3,
        out_specs=vmem,
        compiler_params=params,
        name="pack",
    )(cells, keep, taken)
    second_recv = exchange(second_send)
    mine = pl.pallas_call(
        functools.partial(adapter_kernel, offset=cell_rows + bias_chunk),
        out_shape=jax.ShapeDtypeStruct((adapter_rows // 2, channels), f32),
        in_specs=[vmem],
        out_specs=vmem,
        compiler_params=params,
        name="adapters",
    )(second_recv)
    theirs = swap_cores(mine)
    pair_grad = pl.pallas_call(
        after_kernel,
        out_shape=jax.ShapeDtypeStruct((own, count, channels), bf16),
        in_specs=[vmem] * 5,
        out_specs=vmem,
        scratch_shapes=[
            pltpu.VMEM((total, channels), f32),
            pltpu.VMEM((total, channels), f32),
            pltpu.VMEM((bias_chunk, lanes), f32),
        ],
        compiler_params=params,
        cost_estimate=pl.CostEstimate(
            flops=20 * total * channels, bytes_accessed=20 * total * channels, transcendentals=0
        ),
        name="after",
    )(second_recv, unit, inverse, gain_kept, bias_weight_kept)
    down_grad, up_grad = pl.pallas_call(
        final_kernel,
        out_shape=(jax.ShapeDtypeStruct((adapter_rows // 2, channels), f32),) * 2,
        in_specs=[vmem] * 2,
        out_specs=(vmem,) * 2,
        compiler_params=params,
        name="final",
    )(mine, theirs)
    return (
        pair_grad,
        jnp.swapaxes(down_grad.reshape(4, rank, channels), 1, 2),
        up_grad.reshape(4, rank, channels),
    )


def solution(mesh):
    return jax.shard_map(
        local,
        mesh=mesh,
        in_specs=(
            P(("groups", "dap", "sub"), None, None),
            P(("groups", "dap", "sub"), None, None),
            P("groups"),
            P("groups"),
            P(),
            P(),
            P(),
            P(),
            P(),
            P(),
            P(),
        ),
        out_specs=(
            P(("groups", "dap", "sub"), None, None),
            P("groups", None, None),
            P("groups", None, None),
        ),
        check_vma=False,
    )
```

```python
import functools
import math

import jax
import jax.numpy as jnp
from jax import lax
from jax.experimental import pallas as pl
from jax.experimental.pallas import tpu as pltpu
from jax.sharding import PartitionSpec as P

epsilon = 1e-05
lanes = 128
block = 256
masked_bias = -3e38
together = 4
group_axes = ("dap", "sub")
vmem = pl.BlockSpec(memory_space=pltpu.VMEM)
hbm = pl.BlockSpec(memory_space=pltpu.HBM)


def nn(left, right):
    return jnp.dot(left, right, preferred_element_type=jnp.float32)


def nt(left, right):
    return lax.dot_general(left, right, (((1,), (1,)), ((), ())), preferred_element_type=jnp.float32)


def tn(left, right):
    return lax.dot_general(left, right, (((0,), (0,)), ((), ())), preferred_element_type=jnp.float32)


def half(values):
    return values.astype(jnp.bfloat16)


def repeat(count, body):
    if count == 1:
        body(0)
    else:
        lax.fori_loop(0, count, lambda step, carry: (body(step), carry)[1], 0)


def before_kernel(
    mask_hbm, label_hbm, label_row_hbm, pair_hbm, cot_hbm, gain_hbm, bias_weight_hbm, table_hbm,
    send_ref, unit_ref, inverse_ref, gain_ref, bias_weight_ref,
    normed_ref, cells_ref, bias_ref, mask_ref, label_ref, label_row_ref, pair_ref, cot_ref, table_ref, sems,
):
    copies = [
        pltpu.make_async_copy(source, target, sems.at[index])
        for index, (source, target) in enumerate((
            (pair_hbm, pair_ref), (mask_hbm, mask_ref), (label_hbm, label_ref), (label_row_hbm, label_row_ref),
            (gain_hbm, gain_ref), (bias_weight_hbm, bias_weight_ref), (table_hbm, table_ref), (cot_hbm, cot_ref),
        ))
    ]
    for copy in copies:
        copy.start()
    for copy in copies[1:-1]:
        copy.wait()
    own, count, channels = pair_ref.shape
    peers = count // own
    heads, bins = table_ref.shape
    reach = (bins - 2) // 2
    first = lax.axis_index(group_axes) * own
    bias_rows = heads * count // lanes
    gain = gain_ref[...]
    key_pos = lax.broadcasted_iota(jnp.int32, (1, count), 1)
    bin_ids = lax.broadcasted_iota(jnp.int32, (bins, count), 0)
    table = table_ref[...]
    table_parts = []
    for _ in range(3):
        table_parts.append(half(table))
        table = table - table_parts[-1].astype(jnp.float32)
    table_parts = jnp.concatenate(table_parts, axis=0)

    def relative_bias(here):
        same = label_row_ref[...] == label_ref[here]
        offset = jnp.clip(here - key_pos, -reach, reach) + reach
        onehot = half((bin_ids == jnp.where(same, offset, bins - 1)).astype(jnp.float32))
        found = nn(table_parts, onehot)
        return found[:heads] + found[heads : 2 * heads] + found[2 * heads :]

    relative = [relative_bias(first + row) for row in range(own)]
    copies[0].wait()
    for row in range(own):
        here = first + row
        values = pair_ref[row].astype(jnp.float32)
        centred = values - jnp.mean(values, axis=-1, keepdims=True)
        inverse = lax.rsqrt(jnp.mean(centred * centred, axis=-1, keepdims=True) + epsilon)
        unit = centred * inverse
        normed = unit * gain
        unit_ref[row * count : (row + 1) * count] = unit
        inverse_ref[row * count : (row + 1) * count] = inverse
        normed_ref[row * count : (row + 1) * count] = normed
        bias = half(nt(bias_weight_ref[...], half(normed)) + relative[row]).astype(jnp.float32)
        bias = jnp.where(mask_ref[here] > 0, bias, masked_bias)
        for head in range(heads):
            if count < lanes:
                each = lanes // count
                place = (head % each) * count
                bias_ref[row * bias_rows + head // each, place : place + count] = bias[head]
            else:
                for part in range(count // lanes):
                    bias_ref[row * bias_rows + head * (count // lanes) + part, :] = bias[
                        head, part * lanes : (part + 1) * lanes
                    ]
    cell_rows = own * own

    def scatter():
        for row in range(own):
            for place in range(own):
                cells_ref[pl.ds(row * own + place, peers, stride=cell_rows)] = normed_ref[
                    pl.ds(row * count + place, peers, stride=own)
                ]
        return half(cells_ref[...]).reshape(peers, cell_rows, channels)

    send_ref[:, 0:cell_rows] = scatter()
    copies[-1].wait()
    for row in range(own):
        normed_ref[row * count : (row + 1) * count] = cot_ref[row].astype(jnp.float32)
    send_ref[:, cell_rows : 2 * cell_rows] = scatter()
    bias_all = half(bias_ref[...])
    send_ref[:, 2 * cell_rows :] = jnp.broadcast_to(bias_all[None], (peers, *bias_all.shape))


def stacked(maps_ref, count):
    return jnp.concatenate([maps_ref[index] for index in range(count)], axis=0)


def blocked(maps_ref, count):
    empty = jnp.zeros_like(maps_ref[0])
    return jnp.concatenate(
        [
            jnp.concatenate([maps_ref[index] if place == index else empty for place in range(count)], axis=1)
            for index in range(count)
        ],
        axis=0,
    )


def beside(weight_ref, first):
    return jnp.concatenate([weight_ref[first], weight_ref[first + 1]], axis=1)


def adapter_half(given, target_ref, x_ref, u_ref, gate_ref, att_ref, dprojs_ref, down_ref, up_ref):
    total, channels = x_ref.shape
    rank = down_ref.shape[1]
    steps = total // block
    first = lax.rem(lax.axis_index("sub"), 2) == 0
    if steps > 1:
        target_ref[...] = jnp.zeros_like(target_ref)

    def upper(x, u, gated, dprojs):
        low = half(nt(stacked(down_ref, 3), x))
        return [
            *[
                nn(low[index * rank : (index + 1) * rank], dprojs[:, index * channels : (index + 1) * channels])
                for index in range(3)
            ],
            nn(half(nt(down_ref[3], gated)), u),
        ]

    def lower(x, u, gated, dprojs):
        return [nn(half(nt(blocked(up_ref, 3), dprojs)), x), nn(half(nt(up_ref[3], u)), gated)]

    def step_of(part):
        def step(index):
            rows = pl.ds(pl.multiple_of(index * block, block), block)
            gated = half(gate_ref[rows] * att_ref[rows])
            found = jnp.concatenate(part(x_ref[rows], u_ref[rows], gated, dprojs_ref[rows]), axis=0)
            target_ref[...] = target_ref[...] + found if steps > 1 else found

        return step

    @pl.when(first == given)
    def _():
        repeat(steps, step_of(upper))

    @pl.when(first != given)
    def _():
        repeat(steps, step_of(lower))


def middle_kernel(
    recv_ref, weight_ref, out_weight_ref, down_ref, up_ref,
    dprojs_ref, x_ref, u_ref, gate_ref, dgated_ref, att_ref, bias_ref, give_ref,
    rows_ref, q_ref, k_ref, v_ref, da_ref, da2_ref, dq_ref, dk_ref, dv_ref, gathered_ref,
    *, own, heads,
):
    peers = recv_ref.shape[0]
    channels = recv_ref.shape[2]
    count = own * peers
    cell_rows = own * own
    width = channels // heads
    scale = 1.0 / math.sqrt(width)
    bias_rows = heads * count // lanes
    total = own * count
    joint = min(count, block)
    joint_heads = block // joint

    for target, offset in ((x_ref, 0), (u_ref, cell_rows)):
        rows_ref[...] = recv_ref[:, offset : offset + cell_rows].astype(jnp.float32).reshape(total, channels)
        for place in range(own):
            target[place * count : (place + 1) * count] = half(rows_ref[pl.ds(place, count, stride=own)])
    gathered = recv_ref[:, 2 * cell_rows :].astype(jnp.float32)
    gathered_ref[...] = gathered.reshape(count * bias_rows, lanes)
    for part in range(bias_rows):
        bias_ref[:, part * lanes : (part + 1) * lanes] = gathered_ref[pl.ds(part, count, stride=bias_rows)]

    downs = stacked(down_ref, 3)
    ups = blocked(up_ref, 3)

    spare = jnp.concatenate([ups[:, 2 * channels :], jnp.zeros_like(ups[:, :channels])], axis=1)

    def project(step):
        rows = pl.ds(pl.multiple_of(step * block, block), block)
        x = x_ref[rows]
        u = u_ref[rows]
        joined = jnp.concatenate([x, half(nt(x, downs))], axis=1)
        pair01 = nn(joined, jnp.concatenate([beside(weight_ref, 0), ups[:, : 2 * channels]], axis=0))
        pair23 = nn(joined, jnp.concatenate([beside(weight_ref, 2), spare], axis=0))
        q_ref[rows] = half(pair01[:, :channels])
        k_ref[rows] = half(pair01[:, channels:])
        v_ref[rows] = half(pair23[:, :channels])
        gate = jax.nn.sigmoid(pair23[:, channels:])
        dgated = nt(u, out_weight_ref[...]) + nn(half(nt(u, up_ref[3])), down_ref[3])
        gate_ref[rows] = gate
        dgated_ref[rows] = dgated
        dattended = dgated * gate
        leading = half(dattended)
        da_ref[rows] = leading
        da2_ref[rows] = half(dattended - leading.astype(jnp.float32))

    repeat(total // block, project)

    head_of = lax.broadcasted_iota(jnp.int32, (1, channels), 1) // width
    blocks = heads * count // block

    def attend(rows, part):
        start = part * block // count
        column = pl.multiple_of(part * block, block)
        first = 0 if count <= block else pl.multiple_of(lax.rem(part * block, count), block)
        queries = [pl.ds(row * count + first, joint) for row in rows]
        keys = [pl.ds(row * count, count) for row in rows]
        spots = [(head_of == start + head).astype(jnp.float32) for head in range(joint_heads)]
        marks = [half(spot) for spot in spots]

        def spread(values):
            return jnp.concatenate([values * mark for mark in marks], axis=0)

        def collect(values):
            pieces = [values[head * joint : (head + 1) * joint] for head in range(joint_heads)]
            if joint_heads < heads:
                return sum(piece * spot for piece, spot in zip(pieces, spots))
            found = pieces[-1]
            for head in range(heads - 1):
                found = jnp.where(head_of == head, pieces[head], found)
            return found

        bias = bias_ref[:, pl.ds(column, block)]
        valid = bias > -1e38
        q_wide = [spread(q_ref[at]) for at in queries]
        da_wide = [jnp.concatenate([spread(da_ref[at]), spread(da2_ref[at])], axis=1) for at in queries]
        k_all = [k_ref[at] for at in keys]
        v_all = [v_ref[at] for at in keys]
        scores = [
            jnp.where(valid, nt(key, query) * scale + bias, -1000000000.0) for key, query in zip(k_all, q_wide)
        ]
        dchances = [
            half(nt(jnp.concatenate([value, value], axis=1), da)).astype(jnp.float32)
            for value, da in zip(v_all, da_wide)
        ]
        powers = [jnp.exp(each - jnp.max(each, axis=0, keepdims=True)) for each in scores]
        chances = [each * (1.0 / jnp.sum(each, axis=0, keepdims=True)) for each in powers]
        rounded = [half(each) for each in chances]
        att = [collect(tn(each, value)) for each, value in zip(rounded, v_all)]
        dv = [nn(each, da) for each, da in zip(rounded, da_wide)]
        inner = [left * right for left, right in zip(dchances, chances)]
        dscores = [
            jnp.where(valid, left - right * jnp.sum(left, axis=0, keepdims=True), 0.0)
            for left, right in zip(inner, chances)
        ]
        scaled = [each * scale for each in dscores]
        leading = [half(each) for each in scaled]
        both = [
            jnp.concatenate([lead, half(each - lead.astype(jnp.float32))], axis=0)
            for lead, each in zip(leading, scaled)
        ]
        dk = [nn(each, query) for each, query in zip(both, q_wide)]
        dq = [collect(tn(each, jnp.concatenate([key, key], axis=0))) for each, key in zip(both, k_all)]
        dk = [each[:count] + each[count:] for each in dk]
        dv = [each[:, :channels] + each[:, channels:] for each in dv]
        return list(zip(queries, keys, att, dq, dk, dv)), sum(dscores[1:], dscores[0])

    if blocks == 1:
        bias_grad = None
        for row in range(0, own, together):
            results, dscores = attend(range(row, min(row + together, own)), 0)
            for queries, keys, att, dq, dk, dv in results:
                att_ref[queries] = att
                dq_ref[queries] = dq
                dk_ref[keys] = dk
                dv_ref[keys] = dv
            bias_grad = dscores if bias_grad is None else bias_grad + dscores
        bias_ref[...] = bias_grad
    else:
        for ref in (att_ref, dq_ref, dk_ref, dv_ref):
            ref[...] = jnp.zeros_like(ref)

        def each(part):
            def each_row(row, bias_grad):
                ((queries, keys, att, dq, dk, dv),), dscores = attend([row], part)
                att_ref[queries] += att
                dq_ref[queries] += dq
                dk_ref[keys] += dk
                dv_ref[keys] += dv
                return bias_grad + dscores

            bias_grad = lax.fori_loop(0, own, each_row, jnp.zeros((count, block), jnp.float32))
            bias_ref[:, pl.ds(pl.multiple_of(part * block, block), block)] = bias_grad

        repeat(blocks, each)

    def finish(step):
        rows = pl.ds(pl.multiple_of(step * block, block), block)
        for index, ref in enumerate((dq_ref, dk_ref, dv_ref)):
            dprojs_ref[rows, index * channels : (index + 1) * channels] = half(ref[rows])

    repeat(total // block, finish)
    adapter_half(True, give_ref, x_ref, u_ref, gate_ref, att_ref, dprojs_ref, down_ref, up_ref)


def cells_kernel(
    dprojs_ref, x_ref, u_ref, gate_ref, dgated_ref, att_ref, bias_ref, weight_ref, down_ref, up_ref,
    send_ref, keep_ref, rows_ref, cells_ref, bias_rows_ref, *, own
):
    peers = send_ref.shape[0]
    channels = send_ref.shape[2]
    count = own * peers
    cell_rows = own * own
    total = own * count
    bias_rows = bias_ref.shape[1] // lanes
    downs = stacked(down_ref, 3)
    ups = blocked(up_ref, 3)

    def rows_of(step):
        rows = pl.ds(pl.multiple_of(step * block, block), block)
        gate = gate_ref[rows]
        dgate = half(dgated_ref[rows] * att_ref[rows] * (gate * (1.0 - gate)))
        dprojs = dprojs_ref[rows]
        rows_ref[rows] = (
            nt(dprojs[:, : 2 * channels], beside(weight_ref, 0))
            + nt(jnp.concatenate([dprojs[:, 2 * channels :], dgate], axis=1), beside(weight_ref, 2))
            + nn(half(nt(dprojs, ups)), downs)
        )

    repeat(total // block, rows_of)
    adapter_half(False, keep_ref, x_ref, u_ref, gate_ref, att_ref, dprojs_ref, down_ref, up_ref)
    for row in range(own):
        for place in range(own):
            cells_ref[pl.ds(row * own + place, peers, stride=cell_rows)] = rows_ref[
                pl.ds(place * count + row, peers, stride=own)
            ]
    for part in range(bias_rows):
        bias_rows_ref[pl.ds(part, count, stride=bias_rows)] = bias_ref[:, part * lanes : (part + 1) * lanes]
    send_ref[:, 0:cell_rows] = half(cells_ref[...]).reshape(peers, cell_rows, channels)
    send_ref[:, cell_rows:] = half(bias_rows_ref[...]).reshape(peers, own * bias_rows, lanes)


def pack_kernel(cells_ref, keep_ref, taken_ref, send_ref):
    peers, rows, _ = cells_ref.shape
    send_ref[:, :rows] = cells_ref[...]
    summed = half(keep_ref[...] + taken_ref[...])
    quarter = summed.shape[0] // 2
    for peer in range(peers):
        side = peer % 2
        send_ref[peer, rows:] = summed[side * quarter : (side + 1) * quarter]


def adapter_kernel(recv_ref, out_ref, *, offset):
    quarter = out_ref.shape[0] // 2
    for side in range(2):
        total = recv_ref[side, offset:].astype(jnp.float32)
        for peer in range(side + 2, recv_ref.shape[0], 2):
            total = total + recv_ref[peer, offset:].astype(jnp.float32)
        out_ref[side * quarter : (side + 1) * quarter] = total


def final_kernel(mine_ref, theirs_ref, down_ref, up_ref):
    side = lax.rem(lax.axis_index("sub"), 2) == 0
    quarter = mine_ref.shape[0] // 2
    for index, ref in enumerate((down_ref, up_ref)):
        mine = mine_ref[index * quarter : (index + 1) * quarter]
        theirs = theirs_ref[index * quarter : (index + 1) * quarter]
        ref[:quarter] = jnp.where(side, mine, theirs)
        ref[quarter:] = jnp.where(side, theirs, mine)


def after_kernel(
    recv_ref, unit_ref, inverse_ref, gain_ref, bias_weight_ref, out_ref, rows_ref, cells_ref, bias_ref
):
    own, count, channels = out_ref.shape
    peers = count // own
    heads = bias_weight_ref.shape[0]
    cell_rows = own * own
    bias_rows = heads * count // lanes
    cells_ref[...] = recv_ref[:, :cell_rows].astype(jnp.float32).reshape(own * count, channels)
    for row in range(own):
        for place in range(own):
            rows_ref[pl.ds(row * count + place, peers, stride=own)] = cells_ref[
                pl.ds(row * own + place, peers, stride=cell_rows)
            ]
    summed = recv_ref[0, cell_rows : cell_rows + own * bias_rows].astype(jnp.float32)
    for peer in range(1, peers):
        summed = summed + recv_ref[peer, cell_rows : cell_rows + own * bias_rows].astype(jnp.float32)
    bias_ref[...] = summed
    for row in range(own):
        pieces = []
        for head in range(heads):
            if count < lanes:
                each = lanes // count
                place = (head % each) * count
                line = row * bias_rows + head // each
                pieces.append(bias_ref[line : line + 1, place : place + count])
            else:
                parts = count // lanes
                line = row * bias_rows + head * parts
                pieces.append(
                    jnp.concatenate([bias_ref[line + part : line + part + 1] for part in range(parts)], axis=1)
                )
        bias_grad = half(jnp.concatenate(pieces, axis=0))
        rows = slice(row * count, (row + 1) * count)
        unit = unit_ref[rows]
        grad = (rows_ref[rows] + tn(bias_grad, bias_weight_ref[...])) * gain_ref[...]
        along = jnp.mean(grad * unit, axis=-1, keepdims=True)
        result = inverse_ref[rows] * (grad - jnp.mean(grad, axis=-1, keepdims=True) - unit * along)
        out_ref[row] = half(result)


def swap_cores(values):
    size = lax.axis_size("sub")
    return lax.ppermute(values, "sub", [(place, place ^ 1) for place in range(size)])


def exchange(values):
    return lax.all_to_all(values, group_axes, split_axis=0, concat_axis=0, tiled=True)


def local(
    pair,
    cotangent,
    residue_mask,
    chain_labels,
    gain,
    projection_weight,
    bias_weight,
    output_weight,
    position_bias_table,
    adapter_down_maps,
    adapter_up_maps,
):
    own, count, channels = pair.shape
    peers = count // own
    heads = position_bias_table.shape[0]
    rank = adapter_up_maps.shape[1]
    total = own * count
    cell_rows = own * own
    bias_rows = heads * count // lanes
    adapter_rows = 8 * rank
    adapter_chunk = adapter_rows // 4
    bias_chunk = own * bias_rows
    f32, bf16 = jnp.float32, jnp.bfloat16
    gain_row = gain.reshape(1, channels)
    bias_weight_t = bias_weight.T
    downs = jnp.swapaxes(adapter_down_maps, 1, 2)
    params = pltpu.CompilerParams(vmem_limit_bytes=(16 if total <= 1024 else 56) * 1024 * 1024)

    first_send, unit, inverse, gain_kept, bias_weight_kept = pl.pallas_call(
        before_kernel,
        out_shape=(
            jax.ShapeDtypeStruct((peers, 2 * cell_rows + bias_chunk, channels), bf16),
            jax.ShapeDtypeStruct((total, channels), f32),
            jax.ShapeDtypeStruct((total, 1), f32),
            jax.ShapeDtypeStruct((1, channels), f32),
            jax.ShapeDtypeStruct((heads, channels), bf16),
        ),
        in_specs=[hbm] * 8,
        out_specs=(vmem,) * 5,
        scratch_shapes=[
            pltpu.VMEM((total, channels), f32),
            pltpu.VMEM((total, channels), f32),
            pltpu.VMEM((bias_chunk, lanes), f32),
            pltpu.SMEM((count,), jnp.int32),
            pltpu.SMEM((count,), jnp.int32),
            pltpu.VMEM((1, count), jnp.int32),
            pltpu.VMEM(pair.shape, bf16),
            pltpu.VMEM(pair.shape, bf16),
            pltpu.VMEM(position_bias_table.shape, f32),
            pltpu.SemaphoreType.DMA((8,)),
        ],
        compiler_params=params,
        name="before",
    )(
        *(
            pltpu.with_memory_space_constraint(value, pltpu.HBM)
            for value in (
                residue_mask, chain_labels, chain_labels.reshape(1, count), pair, cotangent, gain_row,
                bias_weight_t, position_bias_table,
            )
        )
    )
    first_recv = exchange(first_send)
    *kept, give = pl.pallas_call(
        functools.partial(middle_kernel, own=own, heads=heads),
        out_shape=(
            jax.ShapeDtypeStruct((total, 3 * channels), bf16),
            *[jax.ShapeDtypeStruct((total, channels), bf16)] * 2,
            *[jax.ShapeDtypeStruct((total, channels), f32)] * 3,
            jax.ShapeDtypeStruct((count, heads * count), f32),
            jax.ShapeDtypeStruct((adapter_rows // 2, channels), f32),
        ),
        in_specs=[vmem] * 5,
        out_specs=(vmem,) * 8,
        scratch_shapes=[
            pltpu.VMEM((total, channels), f32),
            *[pltpu.VMEM((total, channels), bf16)] * 5,
            *[pltpu.VMEM((total, channels), f32)] * 3,
            pltpu.VMEM((count * bias_rows, lanes), f32),
        ],
        compiler_params=params,
        name="middle",
    )(first_recv, projection_weight, output_weight, downs, adapter_up_maps)
    taken = swap_cores(give)
    cells, keep = pl.pallas_call(
        functools.partial(cells_kernel, own=own),
        out_shape=(
            jax.ShapeDtypeStruct((peers, cell_rows + bias_chunk, channels), bf16),
            jax.ShapeDtypeStruct((adapter_rows // 2, channels), f32),
        ),
        in_specs=[vmem] * 10,
        out_specs=(vmem,) * 2,
        scratch_shapes=[
            pltpu.VMEM((total, channels), f32),
            pltpu.VMEM((total, channels), f32),
            pltpu.VMEM((count * bias_rows, lanes), f32),
        ],
        compiler_params=params,
        cost_estimate=pl.CostEstimate(
            flops=10 * total * channels * channels, bytes_accessed=40 * total * channels, transcendentals=0
        ),
        name="cells",
    )(*kept, projection_weight, downs, adapter_up_maps)
    second_send = pl.pallas_call(
        pack_kernel,
        out_shape=jax.ShapeDtypeStruct((peers, cell_rows + bias_chunk + adapter_chunk, channels), bf16),
        in_specs=[vmem] * 3,
        out_specs=vmem,
        compiler_params=params,
        name="pack",
    )(cells, keep, taken)
    second_recv = exchange(second_send)
    mine = pl.pallas_call(
        functools.partial(adapter_kernel, offset=cell_rows + bias_chunk),
        out_shape=jax.ShapeDtypeStruct((adapter_rows // 2, channels), f32),
        in_specs=[vmem],
        out_specs=vmem,
        compiler_params=params,
        name="adapters",
    )(second_recv)
    theirs = swap_cores(mine)
    pair_grad = pl.pallas_call(
        after_kernel,
        out_shape=jax.ShapeDtypeStruct((own, count, channels), bf16),
        in_specs=[vmem] * 5,
        out_specs=vmem,
        scratch_shapes=[
            pltpu.VMEM((total, channels), f32),
            pltpu.VMEM((total, channels), f32),
            pltpu.VMEM((bias_chunk, lanes), f32),
        ],
        compiler_params=params,
        cost_estimate=pl.CostEstimate(
            flops=20 * total * channels, bytes_accessed=20 * total * channels, transcendentals=0
        ),
        name="after",
    )(second_recv, unit, inverse, gain_kept, bias_weight_kept)
    down_grad, up_grad = pl.pallas_call(
        final_kernel,
        out_shape=(jax.ShapeDtypeStruct((adapter_rows // 2, channels), f32),) * 2,
        in_specs=[vmem] * 2,
        out_specs=(vmem,) * 2,
        compiler_params=params,
        name="final",
    )(mine, theirs)
    return (
        pair_grad,
        jnp.swapaxes(down_grad.reshape(4, rank, channels), 1, 2),
        up_grad.reshape(4, rank, channels),
    )


def solution(mesh):
    return jax.shard_map(
        local,
        mesh=mesh,
        in_specs=(
            P(("groups", "dap", "sub"), None, None),
            P(("groups", "dap", "sub"), None, None),
            P("groups"),
            P("groups"),
            P(),
            P(),
            P(),
            P(),
            P(),
            P(),
            P(),
        ),
        out_specs=(
            P(("groups", "dap", "sub"), None, None),
            P("groups", None, None),
            P("groups", None, None),
        ),
        check_vma=False,
    )
```
